32 devices in a mesh: segment: 4 (over y, x), dev: 8 (over z, core).
Axes of the slice: x: 2, y: 2, z: 4, core: 2. Of those that a mesh axis runs over, the one named last changes fastest.
Arguments:
- hidden: bfloat16 [4, 64, 8192], P('segment', 'dev'), may hold values from -6 to 6
- gain: float32 [4, 8192], P('segment'), may hold values from 0.5 to 1.5
- w_query: bfloat16 [4, 8192, 4096], P('segment', None, 'dev'), may hold values from -0.0625 to 0.0625
- w_key: bfloat16 [4, 8192, 512], P('segment', None, 'dev'), may hold values from -0.25 to 0.25
- w_value: bfloat16 [4, 8192, 512], P('segment', None, 'dev'), may hold values from -0.0625 to 0.0625
- w_out: bfloat16 [4, 4096, 8192], P('segment', None, 'dev'), may hold values from -0.09375 to 0.09375
- cache: bfloat16 [4, 32, 128, 1024], P('segment', 'dev'), may hold values from -128 to 128
- block_slot: int32 [32], replicated, may hold values from 0 to 31, as said below
- retrieved: int32 [4, 8, 6], P('segment', 'dev'), may hold values from 0 to 31, as said below
- counts: int32 [4, 8], P('segment', 'dev'), may hold values from 1 to 6, 36 in all within a row
Outputs:
- next_hidden: bfloat16 [4, 64, 8192], P('segment', 'dev')
The draws below stay inside these ranges and needn't reach their ends.
Inputs may be any that keep to these rules, and one draw needn't show every extreme that they name: A permutation: block b lies in row block_slot[b] % 4 of the cache rows held by device block_slot[b] // 4 of dev. `retrieved`: passage block ids; the 6 entries of one request lie on 6 different devices of dev.
All inputs are finite; a program needn't handle non-finite values. No bound on the sum of `counts` on one device may be relied on, other than what follows from the above.
Results may differ from the reference program's by a relative error of at most 0.007.
The reference program's roundings to bfloat16 on the way (of `normed`, `projected`, `weights` and `context`) count: a program that leaves them out, or rounds other values in their place, can miss the bound.
Values may be sent and summed in bfloat16 or wider, within the bound.
No kernel may reach another device: no remote copies, remote signals or barrier semaphores. Data moves between devices by JAX's collectives and lax.ppermute only.
A program may use at most 128 MiB of HBM per device.

```python
import math
import jax
import jax.numpy as jnp
import numpy as np
from jax import lax

D = 8192
HEADS = 32
KV_HEADS = 4
HEAD_DIM = 128
BLK = 128
QLEN = 8
BLK_DEV = 4
REQUESTS = 8
TOKENS = 64
NBLK = 32
TOPK = 6
N_SEGMENT = 4


def slot_order(key):
    spread = jax.random.randint(jax.random.fold_in(key, 7), (NBLK,), 0, 1 << 16)
    return jnp.argsort(spread * NBLK + jnp.arange(NBLK)).astype(jnp.int32)


def draw_block_slot(key, part):
    return slot_order(key)


def draw_retrieved(key, part):
    block_slot = slot_order(key)
    block_at = jnp.argsort(block_slot).astype(jnp.int32)
    owner_total = NBLK // BLK_DEV
    ranking = jax.random.randint(jax.random.fold_in(key, 8), (N_SEGMENT, REQUESTS, owner_total), 0, 1 << 16)
    owners = jnp.argsort(ranking * owner_total + jnp.arange(owner_total), axis=-1)[:, :, :TOPK]
    local_row = jax.random.randint(jax.random.fold_in(key, 9), (N_SEGMENT, REQUESTS, TOPK), 0, BLK_DEV)
    return block_at[owners * BLK_DEV + local_row].astype(jnp.int32)


def draw_cache(key, part):
    full_shape = (N_SEGMENT, NBLK, BLK, 2 * KV_HEADS * HEAD_DIM)
    column = jnp.arange(2 * KV_HEADS * HEAD_DIM)
    is_key = column < KV_HEADS * HEAD_DIM
    spread = jnp.where(is_key, 2.5, 1.5)
    sampled = jnp.clip(jax.random.normal(jax.random.fold_in(key, 3), full_shape, jnp.float32), -6.0, 6.0)
    return (sampled * spread).astype(jnp.bfloat16)


def steps_of(own_key, extent, split, smallest, top_value):
    def one(dim, parts):
        heights = jax.random.uniform(jax.random.fold_in(jax.random.fold_in(own_key, 6), dim), (parts,), jnp.float32, smallest / len(split), top_value / len(split))
        return jnp.repeat(jnp.exp(heights), extent[dim] // parts).reshape((-1,) + (1,) * (len(extent) - dim - 1))

    loudness = one(*split[0])
    for cut in split[1:]:
        loudness = loudness * one(*cut)
    return loudness


def length_profile(amount, total, most, slope):
    portions = [(1 << 20) // math.isqrt(grade ** slope) + 1 for grade in range(2, amount + 1)]
    rest, given = total - most - (amount - 1), [1] * (amount - 1)
    while rest > 0:
        free = [i for i in range(amount - 1) if given[i] < most]
        pool, remaining = sum([portions[i] for i in free]), rest
        for i in free:
            addition = min(most - given[i], max(1, remaining * portions[i] // pool), rest)
            given[i] = given[i] + addition
            rest = rest - addition
    return np.array([most] + given)


def ragged(rng, count, total, reach, skew):
    if count == 2:
        one = jax.random.randint(rng, (), max(1, total - reach), min(reach, total - 1) + 1)
        return jnp.stack([one, total - one])
    tallies = jnp.asarray(length_profile(count, total, reach, skew), jnp.int32)
    twos = (count - 1) // 2
    source_of, receiver = tallies[1:1 + 2 * twos:2], tallies[2:2 + 2 * twos:2]
    margin = jnp.minimum(source_of - 1, reach - receiver)
    moved = jax.random.randint(jax.random.fold_in(rng, 1), (twos,), 0, 1 << 20) % (margin + 1)
    tallies = tallies.at[1:1 + 2 * twos:2].set(source_of - moved).at[2:2 + 2 * twos:2].set(receiver + moved)
    return tallies[jax.random.permutation(jax.random.fold_in(rng, 2), count)]


def noise(own_key, extent, scale, most, shards=(), kind=jnp.bfloat16):
    factor_of = steps_of(own_key, extent, shards, -0.22, 0.18) if shards else 1.0
    array = jax.random.normal(own_key, extent, jnp.float32) * scale * factor_of
    return jnp.minimum(jnp.maximum(array, -most), most).astype(kind)


def setup_inputs(seed: int = 0) -> dict:
    keys = jax.random.split(jax.random.key(seed), 11)
    return {
        "hidden": noise(keys[0], (N_SEGMENT, TOKENS, D), 1.0, 6.0, ((0, 4), (1, 8))),
        "gain": jnp.clip(1.0 + 0.1 * jax.random.normal(keys[1], (N_SEGMENT, D), jnp.float32), 0.5, 1.5),
        "w_query": noise(keys[2], (N_SEGMENT, D, HEADS * HEAD_DIM), D ** -0.5, 0.0625, ((0, 4), (2, 8))),
        "w_key": noise(keys[3], (N_SEGMENT, D, KV_HEADS * HEAD_DIM), (D // 16) ** -0.5, 0.25, ((0, 4), (2, 8))),
        "w_value": noise(keys[4], (N_SEGMENT, D, KV_HEADS * HEAD_DIM), D ** -0.5, 0.0625, ((0, 4), (2, 8))),
        "w_out": noise(keys[5], (N_SEGMENT, HEADS * HEAD_DIM, D), (HEADS * HEAD_DIM) ** -0.5, 0.09375, ((0, 4), (2, 8))),
        "cache": draw_cache(jax.random.fold_in(keys[10], 71), 0),
        "block_slot": draw_block_slot(jax.random.fold_in(keys[10], 71), 0),
        "retrieved": draw_retrieved(jax.random.fold_in(keys[10], 71), 0),
        "counts": jax.vmap(lambda own: ragged(own, REQUESTS, REQUESTS * TOPK * 3 // 4, TOPK, 2))(jax.random.split(keys[9], N_SEGMENT)).reshape((N_SEGMENT, REQUESTS)).astype(jnp.int32),
    }


far_below = -1e+30
norm_eps = 1e-05

def block_stats(scores, valid):
    block_top = lax.optimization_barrier(jnp.max(scores, axis=-1))
    weights = jnp.exp(scores - block_top[..., None])
    block_total = lax.optimization_barrier(jnp.sum(weights, axis=-1))
    live_mask = valid[:, None, None, None]
    block_top = jnp.where(live_mask, block_top, far_below)
    block_total = jnp.where(live_mask, block_total, 0.0)
    return (block_top, block_total, weights.astype(jnp.bfloat16))

def self_stats(queries, key_rows, value_rows, score_scale):
    scores = jnp.einsum('qhgd,khd->qhgk', queries.astype(jnp.float32), key_rows.astype(jnp.float32)) * score_scale
    row_count = queries.shape[0]
    causal = (jnp.arange(row_count)[None, :] <= jnp.arange(row_count)[:, None])[:, None, None, :]
    own_top = lax.optimization_barrier(jnp.max(jnp.where(causal, scores, far_below), axis=-1))
    weights = jnp.where(causal, jnp.exp(scores - own_top[..., None]), 0.0)
    own_total = lax.optimization_barrier(jnp.sum(weights, axis=-1))
    own_acc = jnp.einsum('qhgk,khd->qhgd', weights.astype(jnp.bfloat16).astype(jnp.float32), value_rows.astype(jnp.float32))
    return (own_top, own_total, own_acc)

def combine_terms(block_top, block_total, block_acc, own_top, own_total, own_acc):
    row_peak = jnp.maximum(own_top, lax.optimization_barrier(jnp.max(block_top, axis=0)))
    block_scale = jnp.exp(block_top - row_peak)
    own_scale = jnp.exp(own_top - row_peak)
    numerator = own_acc * own_scale[..., None] + lax.optimization_barrier(jnp.sum(block_acc * block_scale[..., None], axis=0))
    denominator = own_total * own_scale + lax.optimization_barrier(jnp.sum(block_total * block_scale, axis=0))
    return (numerator / denominator[..., None]).astype(jnp.bfloat16)

def segment_layer(hidden, gain, w_query, w_key, w_value, w_out, cache, block_slot, retrieved, counts):
    group_size = HEADS // KV_HEADS
    score_scale = HEAD_DIM ** (-0.5)
    pair_width = KV_HEADS * HEAD_DIM
    query_width = HEADS * HEAD_DIM
    state = hidden.astype(jnp.float32)
    inverse = lax.rsqrt(lax.optimization_barrier(jnp.mean(state * state, axis=-1, keepdims=True)) + norm_eps)
    normed = (state * inverse * gain.astype(jnp.float32)).astype(jnp.bfloat16)
    stacked = jnp.concatenate([w_query, w_key, w_value], axis=1)
    projected = jnp.dot(normed, stacked, preferred_element_type=jnp.float32).astype(jnp.bfloat16)
    queries = projected[:, :query_width].reshape(REQUESTS, QLEN, KV_HEADS, group_size, HEAD_DIM)
    own_keys = projected[:, query_width:query_width + pair_width].reshape(REQUESTS, QLEN, KV_HEADS, HEAD_DIM)
    own_values = projected[:, query_width + pair_width:].reshape(REQUESTS, QLEN, KV_HEADS, HEAD_DIM)

    def one_request(inputs):
        query_rows, key_rows, value_rows, block_ids, live_count = inputs
        slot_ids = block_slot[block_ids].astype(jnp.int32)
        blocks = cache[slot_ids]
        live_mask = jnp.arange(TOPK, dtype=jnp.int32) < live_count
        block_keys = blocks[:, :, :pair_width].reshape(TOPK, BLK, KV_HEADS, HEAD_DIM).astype(jnp.float32)
        block_values = blocks[:, :, pair_width:].reshape(TOPK, BLK, KV_HEADS, HEAD_DIM).astype(jnp.float32)
        scores = jnp.einsum('qhgd,tbhd->tqhgb', query_rows.astype(jnp.float32), block_keys) * score_scale
        block_top, block_total, weights = block_stats(scores, live_mask)
        block_acc = jnp.einsum('tqhgb,tbhd->tqhgd', weights.astype(jnp.float32), block_values)
        block_acc = jnp.where(live_mask[:, None, None, None, None], block_acc, 0.0)
        own_top, own_total, own_acc = self_stats(query_rows, key_rows, value_rows, score_scale)
        return combine_terms(block_top, block_total, block_acc, own_top, own_total, own_acc)
    context = lax.map(one_request, (queries, own_keys, own_values, retrieved, counts))
    context = context.reshape(TOKENS, query_width)
    branch = jnp.dot(context, w_out, preferred_element_type=jnp.float32)
    return (state + branch).astype(jnp.bfloat16)

def reference(hidden, gain, w_query, w_key, w_value, w_out, cache, block_slot, retrieved, counts):
    results = []
    for segment_index in range(N_SEGMENT):
        results.append(segment_layer(hidden[segment_index], gain[segment_index], w_query[segment_index], w_key[segment_index], w_value[segment_index], w_out[segment_index], cache[segment_index], block_slot, retrieved[segment_index], counts[segment_index]))
    return jnp.roll(jnp.stack(results), 1, axis=0)
```

```python
import functools

import jax
import jax.numpy as jnp
from jax import lax
from jax.experimental import pallas as pl
from jax.experimental.pallas import tpu as pltpu
from jax.sharding import PartitionSpec as P

HEADS = 32
KV_HEADS = 4
HEAD_DIM = 128


far_below = -1e30
norm_eps = 1e-05


def passed_along(shard, axis, by):
    size = lax.axis_size(axis)
    return lax.ppermute(shard, axis, [(i, (i + by) % size) for i in range(size)])


def lookup_slots(block_ids, block_slot):
    table_width = block_slot.shape[0]
    matches = block_ids[..., None] == jnp.arange(table_width, dtype=jnp.int32)
    return jnp.sum(jnp.where(matches, block_slot, 0), axis=-1)


def block_stats(scores, valid):
    block_top = jnp.max(scores, axis=-1)
    weights = jnp.exp(scores - block_top[..., None])
    block_total = jnp.sum(weights, axis=-1)
    live_mask = valid[:, None, None, None]
    block_top = jnp.where(live_mask, block_top, far_below)
    block_total = jnp.where(live_mask, block_total, 0.0)
    return (block_top, block_total, weights.astype(jnp.bfloat16))


def self_stats(queries, key_rows, value_rows, score_scale):
    scores = (
        jnp.einsum("qhgd,khd->qhgk", queries, key_rows, preferred_element_type=jnp.float32)
        * score_scale
    )
    row_count = queries.shape[0]
    causal = (jnp.arange(row_count)[None, :] <= jnp.arange(row_count)[:, None])[:, None, None, :]
    own_top = jnp.max(jnp.where(causal, scores, far_below), axis=-1)
    weights = jnp.where(causal, jnp.exp(scores - own_top[..., None]), 0.0)
    own_total = jnp.sum(weights, axis=-1)
    own_acc = jnp.einsum(
        "qhgk,khd->qhgd",
        weights.astype(jnp.bfloat16),
        value_rows,
        preferred_element_type=jnp.float32,
    )
    return (own_top, own_total, own_acc)


def combine_terms(block_top, block_total, block_acc, own_top, own_total, own_acc):
    row_peak = jnp.maximum(own_top, jnp.max(block_top, axis=0))
    block_scale = jnp.exp(block_top - row_peak)
    own_scale = jnp.exp(own_top - row_peak)
    numerator = own_acc * own_scale[..., None] + jnp.sum(block_acc * block_scale[..., None], axis=0)
    denominator = own_total * own_scale + jnp.sum(block_total * block_scale, axis=0)
    return (numerator / denominator[..., None]).astype(jnp.bfloat16)


def general_body(hidden, gain, w_query, w_key, w_value, w_out, cache, block_slot, retrieved, counts):
    devices = lax.axis_size("dev")
    owner_index = lax.axis_index("dev")
    group_size = HEADS // KV_HEADS
    score_scale = HEAD_DIM ** (-0.5)
    pair_width = KV_HEADS * HEAD_DIM
    query_width = HEADS * HEAD_DIM
    state = hidden[0].astype(jnp.float32)
    inverse = lax.rsqrt(jnp.mean(state * state, axis=-1, keepdims=True) + norm_eps)
    normed = (state * inverse * gain[0]).astype(jnp.bfloat16)
    stacked = jnp.concatenate([w_query[0], w_key[0], w_value[0]], axis=1)
    query_cols = w_query.shape[2]
    key_cols = w_key.shape[2]
    projected = jnp.dot(
        lax.all_gather(normed, "dev", axis=0, tiled=True),
        stacked,
        preferred_element_type=jnp.float32,
    ).astype(jnp.bfloat16)
    query_part = projected[:, :query_cols]
    key_part = projected[:, query_cols : query_cols + key_cols]
    value_part = projected[:, query_cols + key_cols :]
    query_flat, key_flat, value_flat = (
        lax.all_to_all(query_part, "dev", split_axis=0, concat_axis=1, tiled=True),
        lax.all_to_all(key_part, "dev", split_axis=0, concat_axis=1, tiled=True),
        lax.all_to_all(value_part, "dev", split_axis=0, concat_axis=1, tiled=True),
    )
    question = query_flat.shape[0]
    queries = query_flat.reshape(question, KV_HEADS, group_size, HEAD_DIM)
    own_keys = key_flat.reshape(question, KV_HEADS, HEAD_DIM)
    own_values = value_flat.reshape(question, KV_HEADS, HEAD_DIM)
    all_ids, all_counts = (
        lax.all_gather(retrieved[0], "dev", axis=0, tiled=True),
        lax.all_gather(counts[0], "dev", axis=0, tiled=True),
    )
    table_rows = cache.shape[1]
    slot_ids = lookup_slots(all_ids, block_slot)
    listed = jnp.arange(all_ids.shape[1], dtype=jnp.int32)[None, :] < all_counts[:, None]
    mine = listed & (slot_ids // table_rows == owner_index)
    local_row = slot_ids % table_rows
    picked = jnp.sum(
        (
            mine[:, :, None] & (local_row[:, :, None] == jnp.arange(table_rows, dtype=jnp.int32))
        ).astype(jnp.bfloat16),
        axis=1,
    )
    selected = jnp.einsum(
        "rb,btc->rtc", picked, cache[0], preferred_element_type=jnp.float32
    ).astype(jnp.bfloat16)
    own_top, own_total, own_acc = self_stats(queries, own_keys, own_values, score_scale)
    my_slots = lookup_slots(retrieved[0][0], block_slot)
    my_listed = jnp.arange(retrieved.shape[2], dtype=jnp.int32) < counts[0][0]
    owner_ids = jnp.arange(devices, dtype=jnp.int32)
    holders = jnp.any(
        my_listed[None, :] & (my_slots[None, :] // table_rows == owner_ids[:, None]), axis=1
    )
    arrived = lax.all_to_all(selected, "dev", split_axis=0, concat_axis=0, tiled=True)
    arrived_keys = arrived[:, :, :pair_width].reshape(devices, -1, KV_HEADS, HEAD_DIM)
    arrived_values = arrived[:, :, pair_width:].reshape(devices, -1, KV_HEADS, HEAD_DIM)
    scores = (
        jnp.einsum("qhgd,tbhd->tqhgb", queries, arrived_keys, preferred_element_type=jnp.float32)
        * score_scale
    )
    block_top, block_total, weights = block_stats(scores, holders)
    block_acc = jnp.einsum(
        "tqhgb,tbhd->tqhgd", weights, arrived_values, preferred_element_type=jnp.float32
    )
    block_acc = jnp.where(holders[:, None, None, None, None], block_acc, 0.0)
    context = combine_terms(block_top, block_total, block_acc, own_top, own_total, own_acc).reshape(
        question, query_width
    )
    branch_cols = jnp.dot(
        lax.all_gather(context, "dev", axis=0, tiled=True),
        w_out[0],
        preferred_element_type=jnp.float32,
    )
    branch = lax.all_to_all(branch_cols, "dev", split_axis=0, concat_axis=1, tiled=True)
    updated = (state + branch).astype(jnp.bfloat16)
    return passed_along(updated[None], "segment", 1)


CORES = 2
VMEM = pl.BlockSpec(memory_space=pltpu.VMEM)
SMEM = pl.BlockSpec(memory_space=pltpu.SMEM)
ANYWHERE = pl.BlockSpec(memory_space=pl.ANY)
MIB = 1 << 20


def to_pair(x, k):
    size = lax.axis_size("dev")
    return lax.ppermute(x, "dev", [(d, (d + CORES * k) % size) for d in range(size)])


def to_partner(x):
    return lax.ppermute(x, "dev", [(d, d ^ 1) for d in range(lax.axis_size("dev"))])


def after(x, *others):
    return lax.optimization_barrier((x, *others))[0]


def matmul(a, b, dims=((1,), (0,))):
    return lax.dot_general(a, b, (dims, ((), ())), preferred_element_type=jnp.float32)


def pack_kernel(place, cache, *rest):
    outs, sems = rest[:-1], rest[-1]
    pairs = len(outs)
    width = cache.shape[3] // 2
    copies = []
    for k in list(range(1, pairs)) + [0]:
        head = lax.rem(place[0] + k, pairs)
        for part in range(2):
            columns = pl.ds(pl.multiple_of(part * width + head * HEAD_DIM, HEAD_DIM), HEAD_DIM)
            copy = pltpu.make_async_copy(
                cache.at[0, :, :, columns], outs[k].at[:, part], sems.at[k, part]
            )
            copy.start()
            copies.append(copy)
    for copy in copies:
        copy.wait()


def pack(place, cache):
    pairs = KV_HEADS
    rows, tokens = cache.shape[1], cache.shape[2]
    shape = jax.ShapeDtypeStruct((rows, 2, tokens, HEAD_DIM), cache.dtype)
    return pl.pallas_call(
        pack_kernel,
        out_shape=[shape] * pairs,
        in_specs=[SMEM, ANYWHERE],
        out_specs=[ANYWHERE] * pairs,
        scratch_shapes=[pltpu.SemaphoreType.DMA((pairs, 2))],
        cost_estimate=pl.CostEstimate(flops=0, bytes_accessed=2 * cache.size * 2, transcendentals=0),
        name="pack",
    )(place, cache)


def project_kernel(place, *refs):
    count = 2 * KV_HEADS
    parts, rest = refs[:count], refs[count:]
    gain, wq, wk, wv, q_out, kv_out, cols_out, normed, wq_vm, wk_vm, wv_vm, sems = rest
    chunks = sems.shape[0] - 2
    depth = wq.shape[1] // chunks
    pair, core = place[0], place[1]
    copies = [
        pltpu.make_async_copy(wk, wk_vm, sems.at[chunks]),
        pltpu.make_async_copy(wv, wv_vm, sems.at[chunks + 1]),
    ]
    for i in range(chunks):
        rows = pl.ds(i * depth, depth)
        copies.append(pltpu.make_async_copy(wq.at[0, rows], wq_vm.at[rows], sems.at[i]))
    for copy in copies:
        copy.start()
    first = core == 0
    columns = pl.ds(pl.multiple_of((CORES * pair + core) * cols_out.shape[1], 128), cols_out.shape[1])
    for k in range(KV_HEADS):
        source = lax.rem(pair + KV_HEADS - k, KV_HEADS)
        rows = pl.ds(pl.multiple_of(source * 16, 16), 16)
        mine, other = parts[2 * k], parts[2 * k + 1]

        def both(at):
            a, b = mine[:, at].astype(jnp.float32), other[:, at].astype(jnp.float32)
            return jnp.concatenate([jnp.where(first, a, b), jnp.where(first, b, a)], axis=0)

        state = both(slice(None))
        inverse = lax.rsqrt(jnp.mean(state * state, axis=-1, keepdims=True) + norm_eps)
        normed[rows, :] = (state * inverse * gain[...]).astype(jnp.bfloat16)
        cols_out[rows, :] = both(columns).astype(cols_out.dtype)
    copies[0].wait()
    key = matmul(normed[...], wk_vm[...], ((1,), (1,)))
    copies[1].wait()
    value = matmul(normed[...], wv_vm[...], ((1,), (1,)))
    kv_out[...] = jnp.concatenate([key, value], axis=1).astype(kv_out.dtype)
    total = jnp.zeros(q_out.shape, jnp.float32)
    for i in range(chunks):
        at = slice(i * depth, (i + 1) * depth)
        copies[2 + i].wait()
        total = total + matmul(normed[:, at], wq_vm[at, :])
    q_out[...] = total.astype(q_out.dtype)


def project(place, parts, gain, wq, wk, wv):
    tokens = sum(p.shape[0] for p in parts)
    width = parts[0].shape[1]
    chunks = 8
    bf16 = jnp.bfloat16
    return pl.pallas_call(
        project_kernel,
        out_shape=[
            jax.ShapeDtypeStruct((tokens, wq.shape[2]), bf16),
            jax.ShapeDtypeStruct((tokens, 2 * wk.shape[0]), bf16),
            jax.ShapeDtypeStruct((tokens, width // len(parts)), bf16),
        ],
        in_specs=[SMEM] + [VMEM] * (len(parts) + 1) + [ANYWHERE] * 3,
        out_specs=[VMEM] * 3,
        scratch_shapes=[
            pltpu.VMEM((tokens, width), bf16),
            pltpu.VMEM(wq.shape[1:], bf16),
            pltpu.VMEM(wk.shape, bf16),
            pltpu.VMEM(wv.shape, bf16),
            pltpu.SemaphoreType.DMA((chunks + 2,)),
        ],
        compiler_params=pltpu.CompilerParams(vmem_limit_bytes=28 * MIB),
        cost_estimate=pl.CostEstimate(
            flops=2 * tokens * width * 640, bytes_accessed=2 * width * 640, transcendentals=0
        ),
        name="project",
    )(place, *parts, gain, wq, wk, wv)


def attend_kernel(place, table, meta, q, kv_mine, kv_other, *refs):
    count = 2 * KV_HEADS
    held, (out, blocks, placed, sems) = refs[:count], refs[count:]
    requests = meta.shape[0]
    listed = meta.shape[1] - 1
    tokens = q.shape[0]
    question = tokens // requests
    heads = q.shape[1] // HEAD_DIM
    group = heads * question
    rows = held[0].shape[0]
    pair, core = place[0], place[1]
    copies = [pltpu.make_async_copy(held[i], blocks.at[i], sems.at[i]) for i in range(count)]
    for copy in copies:
        copy.start()
    scale = HEAD_DIM ** (-0.5)
    first = core == 0
    half = HEAD_DIM // 2
    a, b = kv_mine[...].astype(jnp.float32), kv_other[...].astype(jnp.float32)
    lo, hi = jnp.where(first, a, b), jnp.where(first, b, a)
    own_key = jnp.concatenate([lo[:, :half], hi[:, :half]], axis=1).astype(jnp.bfloat16)
    own_value = jnp.concatenate([lo[:, half:], hi[:, half:]], axis=1).astype(jnp.bfloat16)
    wide = q[...].astype(jnp.float32)
    queries = []
    for r in range(requests):
        piece = wide[r * question : (r + 1) * question]
        queries.append(
            jnp.concatenate(
                [piece[:, h * HEAD_DIM : (h + 1) * HEAD_DIM] for h in range(heads)], axis=0
            ).astype(jnp.bfloat16)
        )
    stacked = jnp.concatenate(queries, axis=0)
    scores = matmul(stacked, own_key, ((1,), (1,))) * scale
    row = lax.broadcasted_iota(jnp.int32, scores.shape, 0)
    column = lax.broadcasted_iota(jnp.int32, scores.shape, 1)
    seen = (row // group == column // question) & (column % question <= row % question)
    own_top = jnp.max(jnp.where(seen, scores, far_below), axis=-1, keepdims=True)
    weights = jnp.where(seen, jnp.exp(scores - own_top), 0.0)
    own_total = jnp.sum(weights, axis=-1, keepdims=True)
    own_acc = matmul(weights.astype(jnp.bfloat16), own_value)
    for copy in copies:
        copy.wait()
    for r in range(requests):
        away = lax.rem(pair - r // CORES + KV_HEADS, KV_HEADS)
        at = CORES * away + lax.rem(r + core, CORES)
        live = meta[at, listed]
        mine = slice(r * group, (r + 1) * group)
        tops, totals, accs = [], [], []
        for k in range(listed):
            slot = table[meta[at, k]]
            owner, line = slot // rows, lax.rem(slot, rows)
            source = CORES * lax.rem(pair - owner // CORES + KV_HEADS, KV_HEADS) + lax.rem(owner + core, CORES)
            part = matmul(queries[r], blocks[source, line, 0], ((1,), (1,))) * scale
            top = jnp.max(part, axis=-1, keepdims=True)
            weights = jnp.exp(part - top)
            total = jnp.sum(weights, axis=-1, keepdims=True)
            accs.append(matmul(weights.astype(jnp.bfloat16), blocks[source, line, 1]))
            tops.append(jnp.where(k < live, top, far_below))
            totals.append(total)
        peak = own_top[mine]
        for top in tops:
            peak = jnp.maximum(peak, top)
        factor = jnp.exp(own_top[mine] - peak)
        numerator, denominator = own_acc[mine] * factor, own_total[mine] * factor
        for k in range(listed):
            factor = jnp.where(k < live, jnp.exp(tops[k] - peak), 0.0)
            numerator = numerator + accs[k] * factor
            denominator = denominator + totals[k] * factor
        context = numerator / denominator
        for h in range(heads):
            placed[r * question : (r + 1) * question, h * HEAD_DIM : (h + 1) * HEAD_DIM] = context[
                h * question : (h + 1) * question
            ]
    out[...] = placed[...].astype(out.dtype)


def attend(place, table, meta, q, kv_mine, kv_other, held):
    return pl.pallas_call(
        attend_kernel,
        out_shape=jax.ShapeDtypeStruct(q.shape, jnp.bfloat16),
        in_specs=[SMEM] * 3 + [VMEM] * 3 + [ANYWHERE] * len(held),
        out_specs=VMEM,
        scratch_shapes=[
            pltpu.VMEM((len(held), *held[0].shape), jnp.bfloat16),
            pltpu.VMEM(q.shape, jnp.float32),
            pltpu.SemaphoreType.DMA((len(held),)),
        ],
        compiler_params=pltpu.CompilerParams(vmem_limit_bytes=16 * MIB),
        cost_estimate=pl.CostEstimate(
            flops=1 << 28, bytes_accessed=2 * MIB, transcendentals=1 << 18
        ),
        name="attend",
    )(place, table, meta, q, kv_mine, kv_other, *held)


def finish_kernel(place, *refs):
    count = 2 * KV_HEADS
    parts, (cols, w_out, keep, give, w_vm, placed, sems) = refs[:count], refs[count:]
    pair, core = place[0], place[1]
    depth = parts[0].shape[1]
    copies, spans = [], []
    for i in range(count):
        source = CORES * lax.rem(pair - i // CORES + KV_HEADS, KV_HEADS) + lax.rem(i + core, CORES)
        span = pl.ds(pl.multiple_of(source * depth, depth), depth)
        copy = pltpu.make_async_copy(w_out.at[0, span], w_vm.at[i], sems.at[i])
        copy.start()
        copies.append(copy)
    total = cols[...].astype(jnp.float32) * 0.0
    for i in range(count):
        copies[i].wait()
        total = total + matmul(parts[i][...], w_vm[i])
    placed[...] = cols[...].astype(jnp.float32) + total
    question = keep.shape[1]
    for z in range(KV_HEADS):
        lo = placed[z * 2 * question : (z * 2 + 1) * question]
        hi = placed[(z * 2 + 1) * question : (z * 2 + 2) * question]
        keep[z] = jnp.where(core == 0, lo, hi).astype(keep.dtype)
        give[z] = jnp.where(core == 0, hi, lo).astype(give.dtype)


def finish(place, parts, cols, w_out):
    count = len(parts)
    tokens, width = cols.shape
    shape = jax.ShapeDtypeStruct((KV_HEADS, tokens // count, width), jnp.bfloat16)
    return pl.pallas_call(
        finish_kernel,
        out_shape=[shape] * 2,
        in_specs=[SMEM] + [VMEM] * (count + 1) + [ANYWHERE],
        out_specs=[VMEM] * 2,
        scratch_shapes=[
            pltpu.VMEM((count, parts[0].shape[1], width), jnp.bfloat16),
            pltpu.VMEM((tokens, width), jnp.float32),
            pltpu.SemaphoreType.DMA((count,)),
        ],
        compiler_params=pltpu.CompilerParams(vmem_limit_bytes=24 * MIB),
        cost_estimate=pl.CostEstimate(
            flops=2 * tokens * w_out.size, bytes_accessed=2 * w_out.size, transcendentals=0
        ),
        name="finish",
    )(place, *parts, cols, w_out)


def place_kernel(place, *refs):
    parts, out = refs[:-1], refs[-1]
    pair, core = place[0], place[1]
    width = parts[0].shape[2]
    for k, part in enumerate(parts):
        for p in range(CORES):
            source = CORES * lax.rem(pair - k + KV_HEADS, KV_HEADS) + lax.rem(core + p, CORES)
            out[0, :, pl.ds(pl.multiple_of(source * width, width), width)] = part[p]


def place_columns(place, parts):
    cores, rows, width = parts[0].shape
    return pl.pallas_call(
        place_kernel,
        out_shape=jax.ShapeDtypeStruct((1, rows, width * cores * len(parts)), jnp.bfloat16),
        in_specs=[SMEM] + [VMEM] * len(parts),
        out_specs=VMEM,
        name="place",
    )(place, *parts)


def by_head(hidden, gain, w_query, w_key, w_value, w_out, cache, block_slot, retrieved, counts):
    size, sections = lax.axis_size("dev"), lax.axis_size("segment")
    me = lax.axis_index("dev")
    pair, core = me // CORES, me % CORES
    place = jnp.stack([pair, core]).astype(jnp.int32)

    state = hidden[0]
    arrived = [state] + [to_pair(state, k) for k in range(1, KV_HEADS)]
    parts = [p for a in arrived for p in (a, to_partner(a))]

    packed = pack(place, cache)
    held = [packed[0]]
    for k in range(1, KV_HEADS):
        mine = packed[k] if k == 1 else after(packed[k], arrived[3])
        held.append(to_pair(mine, k))
    held = [h for a in held for h in (a, to_partner(a))]

    entry = jnp.concatenate([retrieved[0], counts], axis=1)
    entries = [entry] + [to_pair(entry, k) for k in range(1, KV_HEADS)]
    stacked = jnp.concatenate(entries, axis=0)
    both = jnp.stack([stacked, to_partner(stacked)], axis=1)
    meta = both.reshape(size, entry.shape[1])

    q, kv, cols = project(
        place, parts, gain, w_query, w_key[0].swapaxes(0, 1), w_value[0].swapaxes(0, 1)
    )
    context = attend(place, block_slot, meta, q, kv, to_partner(kv), held)
    contexts = [context] + [to_pair(context, k) for k in range(1, KV_HEADS)]
    contexts = [p for a in contexts for p in (a, to_partner(a))]
    keep, give = finish(place, contexts, cols, w_out)
    sent = jnp.stack([keep, to_partner(give)], axis=1)
    final = []
    for k in range(KV_HEADS):
        piece = lax.dynamic_index_in_dim(sent, (pair + k) % KV_HEADS, 0, keepdims=False)
        route = [
            (s * size + d, (s + 1) % sections * size + (d + CORES * k) % size)
            for s in range(sections)
            for d in range(size)
        ]
        final.append(lax.ppermute(piece, ("segment", "dev"), route))
    return place_columns(place, final)


def solution(mesh):
    heads_fit = mesh.shape["dev"] == CORES * KV_HEADS
    return jax.shard_map(
        by_head if heads_fit else general_body,
        mesh=mesh,
        in_specs=(
            P("segment", "dev", None),
            P("segment", None),
            P("segment", None, "dev"),
            P("segment", None, "dev"),
            P("segment", None, "dev"),
            P("segment", None, "dev"),
            P("segment", "dev", None, None),
            P(),
            P("segment", "dev", None),
            P("segment", "dev"),
        ),
        out_specs=P("segment", "dev", None),
        check_vma=False,
    )
```

```python
import functools

import jax
import jax.numpy as jnp
from jax import lax
from jax.experimental import pallas as pl
from jax.experimental.pallas import tpu as pltpu
from jax.sharding import PartitionSpec as P

HEADS = 32
KV_HEADS = 4
HEAD_DIM = 128


far_below = -1e30
norm_eps = 1e-05


def passed_along(shard, axis, by):
    size = lax.axis_size(axis)
    return lax.ppermute(shard, axis, [(i, (i + by) % size) for i in range(size)])


def lookup_slots(block_ids, block_slot):
    table_width = block_slot.shape[0]
    matches = block_ids[..., None] == jnp.arange(table_width, dtype=jnp.int32)
    return jnp.sum(jnp.where(matches, block_slot, 0), axis=-1)


def block_stats(scores, valid):
    block_top = jnp.max(scores, axis=-1)
    weights = jnp.exp(scores - block_top[..., None])
    block_total = jnp.sum(weights, axis=-1)
    live_mask = valid[:, None, None, None]
    block_top = jnp.where(live_mask, block_top, far_below)
    block_total = jnp.where(live_mask, block_total, 0.0)
    return (block_top, block_total, weights.astype(jnp.bfloat16))


def self_stats(queries, key_rows, value_rows, score_scale):
    scores = (
        jnp.einsum("qhgd,khd->qhgk", queries, key_rows, preferred_element_type=jnp.float32)
        * score_scale
    )
    row_count = queries.shape[0]
    causal = (jnp.arange(row_count)[None, :] <= jnp.arange(row_count)[:, None])[:, None, None, :]
    own_top = jnp.max(jnp.where(causal, scores, far_below), axis=-1)
    weights = jnp.where(causal, jnp.exp(scores - own_top[..., None]), 0.0)
    own_total = jnp.sum(weights, axis=-1)
    own_acc = jnp.einsum(
        "qhgk,khd->qhgd",
        weights.astype(jnp.bfloat16),
        value_rows,
        preferred_element_type=jnp.float32,
    )
    return (own_top, own_total, own_acc)


def combine_terms(block_top, block_total, block_acc, own_top, own_total, own_acc):
    row_peak = jnp.maximum(own_top, jnp.max(block_top, axis=0))
    block_scale = jnp.exp(block_top - row_peak)
    own_scale = jnp.exp(own_top - row_peak)
    numerator = own_acc * own_scale[..., None] + jnp.sum(block_acc * block_scale[..., None], axis=0)
    denominator = own_total * own_scale + jnp.sum(block_total * block_scale, axis=0)
    return (numerator / denominator[..., None]).astype(jnp.bfloat16)


def general_body(hidden, gain, w_query, w_key, w_value, w_out, cache, block_slot, retrieved, counts):
    devices = lax.axis_size("dev")
    owner_index = lax.axis_index("dev")
    group_size = HEADS // KV_HEADS
    score_scale = HEAD_DIM ** (-0.5)
    pair_width = KV_HEADS * HEAD_DIM
    query_width = HEADS * HEAD_DIM
    state = hidden[0].astype(jnp.float32)
    inverse = lax.rsqrt(jnp.mean(state * state, axis=-1, keepdims=True) + norm_eps)
    normed = (state * inverse * gain[0]).astype(jnp.bfloat16)
    stacked = jnp.concatenate([w_query[0], w_key[0], w_value[0]], axis=1)
    query_cols = w_query.shape[2]
    key_cols = w_key.shape[2]
    projected = jnp.dot(
        lax.all_gather(normed, "dev", axis=0, tiled=True),
        stacked,
        preferred_element_type=jnp.float32,
    ).astype(jnp.bfloat16)
    query_part = projected[:, :query_cols]
    key_part = projected[:, query_cols : query_cols + key_cols]
    value_part = projected[:, query_cols + key_cols :]
    query_flat, key_flat, value_flat = (
        lax.all_to_all(query_part, "dev", split_axis=0, concat_axis=1, tiled=True),
        lax.all_to_all(key_part, "dev", split_axis=0, concat_axis=1, tiled=True),
        lax.all_to_all(value_part, "dev", split_axis=0, concat_axis=1, tiled=True),
    )
    question = query_flat.shape[0]
    queries = query_flat.reshape(question, KV_HEADS, group_size, HEAD_DIM)
    own_keys = key_flat.reshape(question, KV_HEADS, HEAD_DIM)
    own_values = value_flat.reshape(question, KV_HEADS, HEAD_DIM)
    all_ids, all_counts = (
        lax.all_gather(retrieved[0], "dev", axis=0, tiled=True),
        lax.all_gather(counts[0], "dev", axis=0, tiled=True),
    )
    table_rows = cache.shape[1]
    slot_ids = lookup_slots(all_ids, block_slot)
    listed = jnp.arange(all_ids.shape[1], dtype=jnp.int32)[None, :] < all_counts[:, None]
    mine = listed & (slot_ids // table_rows == owner_index)
    local_row = slot_ids % table_rows
    picked = jnp.sum(
        (
            mine[:, :, None] & (local_row[:, :, None] == jnp.arange(table_rows, dtype=jnp.int32))
        ).astype(jnp.bfloat16),
        axis=1,
    )
    selected = jnp.einsum(
        "rb,btc->rtc", picked, cache[0], preferred_element_type=jnp.float32
    ).astype(jnp.bfloat16)
    own_top, own_total, own_acc = self_stats(queries, own_keys, own_values, score_scale)
    my_slots = lookup_slots(retrieved[0][0], block_slot)
    my_listed = jnp.arange(retrieved.shape[2], dtype=jnp.int32) < counts[0][0]
    owner_ids = jnp.arange(devices, dtype=jnp.int32)
    holders = jnp.any(
        my_listed[None, :] & (my_slots[None, :] // table_rows == owner_ids[:, None]), axis=1
    )
    arrived = lax.all_to_all(selected, "dev", split_axis=0, concat_axis=0, tiled=True)
    arrived_keys = arrived[:, :, :pair_width].reshape(devices, -1, KV_HEADS, HEAD_DIM)
    arrived_values = arrived[:, :, pair_width:].reshape(devices, -1, KV_HEADS, HEAD_DIM)
    scores = (
        jnp.einsum("qhgd,tbhd->tqhgb", queries, arrived_keys, preferred_element_type=jnp.float32)
        * score_scale
    )
    block_top, block_total, weights = block_stats(scores, holders)
    block_acc = jnp.einsum(
        "tqhgb,tbhd->tqhgd", weights, arrived_values, preferred_element_type=jnp.float32
    )
    block_acc = jnp.where(holders[:, None, None, None, None], block_acc, 0.0)
    context = combine_terms(block_top, block_total, block_acc, own_top, own_total, own_acc).reshape(
        question, query_width
    )
    branch_cols = jnp.dot(
        lax.all_gather(context, "dev", axis=0, tiled=True),
        w_out[0],
        preferred_element_type=jnp.float32,
    )
    branch = lax.all_to_all(branch_cols, "dev", split_axis=0, concat_axis=1, tiled=True)
    updated = (state + branch).astype(jnp.bfloat16)
    return passed_along(updated[None], "segment", 1)


CORES = 2
TAIL = 16
VMEM = pl.BlockSpec(memory_space=pltpu.VMEM)
SMEM = pl.BlockSpec(memory_space=pltpu.SMEM)
ANYWHERE = pl.BlockSpec(memory_space=pl.ANY)
HBM = pl.BlockSpec(memory_space=pltpu.HBM)
MIB = 1 << 20


def to_pair(x, k):
    size = lax.axis_size("dev")
    return lax.ppermute(x, "dev", [(d, d ^ (CORES * k)) for d in range(size)])


def to_partner(x):
    return lax.ppermute(x, "dev", [(d, d ^ 1) for d in range(lax.axis_size("dev"))])


def from_all(x):
    arrived = [x] + [to_pair(x, k) for k in range(1, KV_HEADS)]
    return [p for a in arrived for p in (a, to_partner(a))]


def after(x, *others):
    return lax.optimization_barrier((x, *others))[0]


def in_vmem(x):
    return pltpu.with_memory_space_constraint(x, pltpu.VMEM)


def matmul(a, b, dims=((1,), (0,))):
    return lax.dot_general(a, b, (dims, ((), ())), preferred_element_type=jnp.float32)


def load_kernel(count, *refs):
    sources, targets, sems = refs[:count], refs[count : 2 * count], refs[2 * count]
    copies = []
    for i in range(count):
        parts = sems.shape[1]
        depth = targets[i].shape[0] // parts
        for j in range(parts):
            rows = pl.ds(j * depth, depth)
            source = sources[i].at[rows] if len(sources[i].shape) == 2 else sources[i].at[0, rows]
            copies.append(pltpu.make_async_copy(source, targets[i].at[rows], sems.at[i, j]))
    for copy in copies:
        copy.start()
    for copy in copies:
        copy.wait()


def load(*arrays):
    return pl.pallas_call(
        functools.partial(load_kernel, len(arrays)),
        out_shape=[pltpu.VMEM(a.shape[-2:], a.dtype) for a in arrays],
        in_specs=[HBM] * len(arrays),
        out_specs=[VMEM] * len(arrays),
        scratch_shapes=[pltpu.SemaphoreType.DMA((len(arrays), 4))],
        compiler_params=pltpu.CompilerParams(vmem_limit_bytes=2 * MIB),
        cost_estimate=pl.CostEstimate(
            flops=0, bytes_accessed=sum(a.size * 2 for a in arrays), transcendentals=0
        ),
        name="load",
    )(*arrays)


def pack_kernel(place, table, retrieved, counts, cache, *rest):
    outs, (whole, sems) = rest[:-2], rest[-2:]
    lines, tokens = whole.shape[0], whole.shape[1]
    width = whole.shape[2] // 2
    copies = [
        pltpu.make_async_copy(cache.at[0, line], whole.at[line], sems.at[line]) for line in range(lines)
    ]
    for copy in copies:
        copy.start()
    listed = retrieved.shape[2]
    lane = lax.broadcasted_iota(jnp.int32, (TAIL, HEAD_DIM), 1)
    note = jnp.where(lane == listed, counts[0, 0], 0)
    for k in range(listed):
        note = jnp.where(lane == k, table[retrieved[0, 0, k]], note)
    note = note.astype(jnp.float32).astype(jnp.bfloat16)
    for out in outs:
        out[lines * 2 * tokens :, :] = note
    for line in range(lines):
        copies[line].wait()
        for k, out in enumerate(outs):
            head = lax.bitwise_xor(place[0], k)
            for part in range(2):
                columns = pl.ds(pl.multiple_of(part * width + head * HEAD_DIM, HEAD_DIM), HEAD_DIM)
                at = (line * 2 + part) * tokens
                out[at : at + tokens, :] = whole[line, :, columns]


def pack(place, table, retrieved, counts, cache):
    rows, tokens = cache.shape[1], cache.shape[2]
    return pl.pallas_call(
        pack_kernel,
        out_shape=[pltpu.VMEM((rows * 2 * tokens + TAIL, HEAD_DIM), cache.dtype)] * KV_HEADS,
        in_specs=[SMEM] * 4 + [ANYWHERE],
        out_specs=[VMEM] * KV_HEADS,
        scratch_shapes=[
            pltpu.VMEM(cache.shape[1:], cache.dtype),
            pltpu.SemaphoreType.DMA((rows,)),
        ],
        compiler_params=pltpu.CompilerParams(vmem_limit_bytes=6 * MIB),
        cost_estimate=pl.CostEstimate(flops=0, bytes_accessed=2 * cache.size * 2, transcendentals=0),
        name="pack",
    )(place, table, retrieved, counts, cache)


def project_kernel(place, *refs):
    count = 2 * KV_HEADS
    parts, rest = refs[:count], refs[count:]
    gain, wq, wk, wv, q_out, kv_out, cols_out, normed = rest
    pair, core = place[0], place[1]
    first = core == 0
    width = cols_out.shape[1]
    columns = pl.ds(pl.multiple_of((CORES * pair + core) * width, 128), width)
    for k in range(KV_HEADS):
        source = lax.bitwise_xor(pair, k)
        rows = pl.ds(pl.multiple_of(source * 16, 16), 16)

        def both(at):
            a, b = (parts[2 * k + p][:, at].astype(jnp.float32) for p in range(CORES))
            return jnp.concatenate([jnp.where(first, a, b), jnp.where(first, b, a)], axis=0)

        state = both(slice(None))
        inverse = lax.rsqrt(jnp.mean(state * state, axis=-1, keepdims=True) + norm_eps)
        normed[rows, :] = (state * inverse * gain[...]).astype(jnp.bfloat16)
        cols_out[rows, :] = both(columns).astype(cols_out.dtype)
    key = matmul(normed[...], wk[...], ((1,), (1,)))
    value = matmul(normed[...], wv[...], ((1,), (1,)))
    kv_out[...] = jnp.concatenate([key, value], axis=1).astype(kv_out.dtype)
    q_out[...] = matmul(normed[...], wq[...]).astype(q_out.dtype)


def project(place, parts, gain, wq, wk, wv):
    tokens = sum(p.shape[0] for p in parts)
    width = parts[0].shape[1]
    bf16 = jnp.bfloat16
    return pl.pallas_call(
        project_kernel,
        out_shape=[
            pltpu.VMEM((tokens, wq.shape[1]), bf16),
            pltpu.VMEM((tokens, 2 * wk.shape[0]), bf16),
            pltpu.VMEM((tokens, width // len(parts)), bf16),
        ],
        in_specs=[SMEM] + [VMEM] * (len(parts) + 4),
        out_specs=[VMEM] * 3,
        scratch_shapes=[pltpu.VMEM((tokens, width), bf16)],
        compiler_params=pltpu.CompilerParams(vmem_limit_bytes=16 * MIB),
        cost_estimate=pl.CostEstimate(
            flops=2 * tokens * width * 640, bytes_accessed=2 * width * 640, transcendentals=0
        ),
        name="project",
    )(place, *[in_vmem(p) for p in parts], gain, in_vmem(wq), in_vmem(wk), in_vmem(wv))


def attend_kernel(place, q, kv_mine, kv_other, *refs):
    count = 2 * KV_HEADS
    held, (out, blocks, placed, scored, notes, meta, sems, note_sem) = refs[:count], refs[count:]
    requests, listed = scored.shape[:2]
    tokens = q.shape[0]
    question = tokens // requests
    heads = q.shape[1] // HEAD_DIM
    group = heads * question
    block = scored.shape[3]
    rows = (blocks.shape[1] - TAIL) // (2 * block)
    pair, core = place[0], place[1]
    me = CORES * pair + core
    copies = [pltpu.make_async_copy(held[i], blocks.at[i], sems.at[i]) for i in range(count)]
    for copy in copies:
        copy.start()
    scale = HEAD_DIM ** (-0.5)
    first = core == 0
    half = HEAD_DIM // 2
    a, b = kv_mine[...].astype(jnp.float32), kv_other[...].astype(jnp.float32)
    lo, hi = jnp.where(first, a, b), jnp.where(first, b, a)
    own_key = jnp.concatenate([lo[:, :half], hi[:, :half]], axis=1).astype(jnp.bfloat16)
    own_value = jnp.concatenate([lo[:, half:], hi[:, half:]], axis=1).astype(jnp.bfloat16)
    wide = q[...].astype(jnp.float32)
    queries = []
    for r in range(requests):
        piece = wide[r * question : (r + 1) * question]
        queries.append(
            jnp.concatenate(
                [piece[:, h * HEAD_DIM : (h + 1) * HEAD_DIM] for h in range(heads)], axis=0
            ).astype(jnp.bfloat16)
        )
    stacked = jnp.concatenate(queries, axis=0)
    for copy in copies:
        copy.wait()
    tail = slice(rows * 2 * block, rows * 2 * block + TAIL)
    notes[...] = jnp.concatenate(
        [blocks[i, tail, :].astype(jnp.float32)[:1] for i in range(count)], axis=0
    ).astype(jnp.int32)
    noted = pltpu.make_async_copy(notes, meta, note_sem)
    noted.start()
    scores = matmul(stacked, own_key, ((1,), (1,))) * scale
    row = lax.broadcasted_iota(jnp.int32, scores.shape, 0)
    column = lax.broadcasted_iota(jnp.int32, scores.shape, 1)
    seen = (row // group == column // question) & (column % question <= row % question)
    own_top = jnp.max(jnp.where(seen, scores, far_below), axis=-1, keepdims=True)
    weights = jnp.where(seen, jnp.exp(scores - own_top), 0.0)
    own_total = jnp.sum(weights, axis=-1, keepdims=True)
    own_acc = matmul(weights.astype(jnp.bfloat16), own_value)
    noted.wait()
    lives, places = [], []
    for r in range(requests):
        at = lax.bitwise_xor(me, r)
        lives.append(meta[at, listed])
        for k in range(listed):
            slot = meta[at, k]
            source = lax.bitwise_xor(me, slot // rows)
            key_at = pl.multiple_of(lax.rem(slot, rows) * 2 * block, block)
            places.append((source, key_at))
            scored[r, k] = matmul(queries[r], blocks[source, pl.ds(key_at, block), :], ((1,), (1,))) * scale
    scores = scored[...]
    tops = jnp.max(scores, axis=-1, keepdims=True)
    weights = jnp.exp(scores - tops)
    totals = jnp.sum(weights, axis=-1, keepdims=True)
    scored[...] = weights
    for r in range(requests):
        mine = slice(r * group, (r + 1) * group)
        live = lives[r]
        accs, marks = [], []
        for k in range(listed):
            source, key_at = places[r * listed + k]
            values = blocks[source, pl.ds(key_at + block, block), :]
            accs.append(matmul(scored[r, k].astype(jnp.bfloat16), values))
            marks.append(jnp.where(k < live, tops[r, k], far_below))
        peak = own_top[mine]
        for mark in marks:
            peak = jnp.maximum(peak, mark)
        factor = jnp.exp(own_top[mine] - peak)
        numerator, denominator = own_acc[mine] * factor, own_total[mine] * factor
        for k in range(listed):
            factor = jnp.where(k < live, jnp.exp(marks[k] - peak), 0.0)
            numerator = numerator + accs[k] * factor
            denominator = denominator + totals[r, k] * factor
        context = numerator / denominator
        for h in range(heads):
            placed[r * question : (r + 1) * question, h * HEAD_DIM : (h + 1) * HEAD_DIM] = context[
                h * question : (h + 1) * question
            ]
    out[...] = placed[...].astype(out.dtype)


def attend(place, q, kv_mine, kv_other, held, requests, listed, block):
    count = len(held)
    return pl.pallas_call(
        attend_kernel,
        out_shape=pltpu.VMEM(q.shape, jnp.bfloat16),
        in_specs=[SMEM] + [VMEM] * 3 + [ANYWHERE] * count,
        out_specs=VMEM,
        scratch_shapes=[
            pltpu.VMEM((count, *held[0].shape), jnp.bfloat16),
            pltpu.VMEM(q.shape, jnp.float32),
            pltpu.VMEM((requests, listed, q.size // HEAD_DIM // requests, block), jnp.float32),
            pltpu.VMEM((count, HEAD_DIM), jnp.int32),
            pltpu.SMEM((count, HEAD_DIM), jnp.int32),
            pltpu.SemaphoreType.DMA((count,)),
            pltpu.SemaphoreType.DMA,
        ],
        compiler_params=pltpu.CompilerParams(vmem_limit_bytes=16 * MIB),
        cost_estimate=pl.CostEstimate(
            flops=1 << 28, bytes_accessed=2 * MIB, transcendentals=1 << 18
        ),
        name="attend",
    )(place, in_vmem(q), in_vmem(kv_mine), in_vmem(kv_other), *held)


def finish_kernel(place, *refs):
    count = 2 * KV_HEADS
    parts, (cols, w_out, keep, give, placed) = refs[:count], refs[count:]
    pair, core = place[0], place[1]
    me = CORES * pair + core
    depth = parts[0].shape[1]
    total = None
    for i in range(count):
        source = lax.bitwise_xor(me, i)
        span = pl.ds(pl.multiple_of(source * depth, depth), depth)
        product = matmul(parts[i][...], w_out[span, :])
        total = product if total is None else total + product
    placed[...] = cols[...].astype(jnp.float32) + total
    question = keep.shape[1]
    for z in range(KV_HEADS):
        lo = placed[z * 2 * question : (z * 2 + 1) * question]
        hi = placed[(z * 2 + 1) * question : (z * 2 + 2) * question]
        keep[z] = jnp.where(core == 0, lo, hi).astype(keep.dtype)
        give[z] = jnp.where(core == 0, hi, lo).astype(give.dtype)


def finish(place, parts, cols, w_out):
    count = len(parts)
    tokens, width = cols.shape
    shape = pltpu.VMEM((KV_HEADS, tokens // count, width), jnp.bfloat16)
    return pl.pallas_call(
        finish_kernel,
        out_shape=[shape] * 2,
        in_specs=[SMEM] + [VMEM] * (count + 2),
        out_specs=[VMEM] * 2,
        scratch_shapes=[pltpu.VMEM((tokens, width), jnp.float32)],
        compiler_params=pltpu.CompilerParams(vmem_limit_bytes=16 * MIB),
        cost_estimate=pl.CostEstimate(
            flops=2 * tokens * w_out.size, bytes_accessed=2 * w_out.size, transcendentals=0
        ),
        name="finish",
    )(place, *[in_vmem(p) for p in parts], in_vmem(cols), in_vmem(w_out))


def route_kernel(place, keep, got, *outs):
    for k, out in enumerate(outs):
        target = lax.bitwise_xor(place[0], k)
        out[0] = keep[target]
        out[1] = got[target]


def route_pieces(place, keep, got):
    shape = pltpu.VMEM((CORES, *keep.shape[1:]), keep.dtype)
    return pl.pallas_call(
        route_kernel,
        out_shape=[shape] * KV_HEADS,
        in_specs=[SMEM] + [VMEM] * 2,
        out_specs=[VMEM] * KV_HEADS,
        compiler_params=pltpu.CompilerParams(vmem_limit_bytes=4 * MIB),
        name="route",
    )(place, in_vmem(keep), in_vmem(got))


def place_kernel(place, *refs):
    parts, out = refs[:-1], refs[-1]
    me = CORES * place[0] + place[1]
    width = parts[0].shape[2]
    for k, part in enumerate(parts):
        for p in range(CORES):
            source = lax.bitwise_xor(me, CORES * k + p)
            out[0, :, pl.ds(pl.multiple_of(source * width, width), width)] = part[p]


def place_columns(place, parts):
    cores, rows, width = parts[0].shape
    return pl.pallas_call(
        place_kernel,
        out_shape=jax.ShapeDtypeStruct((1, rows, width * cores * len(parts)), jnp.bfloat16),
        in_specs=[SMEM] + [VMEM] * len(parts),
        out_specs=VMEM,
        compiler_params=pltpu.CompilerParams(vmem_limit_bytes=4 * MIB),
        name="place",
    )(place, *[in_vmem(p) for p in parts])


def by_head(hidden, gain, w_query, w_key, w_value, w_out, cache, block_slot, retrieved, counts):
    size, sections = lax.axis_size("dev"), lax.axis_size("segment")
    me = lax.axis_index("dev")
    place = jnp.stack([me // CORES, me % CORES]).astype(jnp.int32)

    state = hidden[0]
    arrived = [state] + [to_pair(state, k) for k in range(1, KV_HEADS)]
    packed = pack(place, block_slot, retrieved, counts, cache)
    wq, wk, wv = load(w_query, w_key[0].swapaxes(0, 1), w_value[0].swapaxes(0, 1))
    arrived = [arrived[0]] + [after(a, wq) for a in arrived[1:]]
    parts = [p for a in arrived for p in (a, to_partner(a))]

    held = [packed[0]]
    for k in range(1, KV_HEADS):
        mine = packed[k] if k < 3 else after(packed[k], arrived[1])
        held.append(to_pair(mine, k))
    held = [h for a in held for h in (a, to_partner(a))]

    q, kv, cols = project(place, parts, gain, wq, wk, wv)
    context = attend(
        place, q, kv, to_partner(kv), held, size, retrieved.shape[2], cache.shape[2]
    )
    keep, give = finish(place, from_all(context), cols, w_out[0])
    pieces = route_pieces(place, keep, to_partner(give))
    final = []
    for k, piece in enumerate(pieces):
        route = [
            (s * size + d, (s + 1) % sections * size + (d ^ (CORES * k)))
            for s in range(sections)
            for d in range(size)
        ]
        final.append(lax.ppermute(piece, ("segment", "dev"), route))
    return place_columns(place, final)


def solution(mesh):
    heads_fit = mesh.shape["dev"] == CORES * KV_HEADS
    return jax.shard_map(
        by_head if heads_fit else general_body,
        mesh=mesh,
        in_specs=(
            P("segment", "dev", None),
            P("segment", None),
            P("segment", None, "dev"),
            P("segment", None, "dev"),
            P("segment", None, "dev"),
            P("segment", None, "dev"),
            P("segment", "dev", None, None),
            P(),
            P("segment", "dev", None),
            P("segment", "dev"),
        ),
        out_specs=P("segment", "dev", None),
        check_vma=False,
    )
```

```python
import functools

import jax
import jax.numpy as jnp
from jax import lax
from jax.experimental import pallas as pl
from jax.experimental.pallas import tpu as pltpu
from jax.sharding import PartitionSpec as P

HEADS = 32
KV_HEADS = 4
HEAD_DIM = 128


far_below = -1e30
norm_eps = 1e-05


def passed_along(shard, axis, by):
    size = lax.axis_size(axis)
    return lax.ppermute(shard, axis, [(i, (i + by) % size) for i in range(size)])


def lookup_slots(block_ids, block_slot):
    table_width = block_slot.shape[0]
    matches = block_ids[..., None] == jnp.arange(table_width, dtype=jnp.int32)
    return jnp.sum(jnp.where(matches, block_slot, 0), axis=-1)


def block_stats(scores, valid):
    block_top = jnp.max(scores, axis=-1)
    weights = jnp.exp(scores - block_top[..., None])
    block_total = jnp.sum(weights, axis=-1)
    live_mask = valid[:, None, None, None]
    block_top = jnp.where(live_mask, block_top, far_below)
    block_total = jnp.where(live_mask, block_total, 0.0)
    return (block_top, block_total, weights.astype(jnp.bfloat16))


def self_stats(queries, key_rows, value_rows, score_scale):
    scores = (
        jnp.einsum("qhgd,khd->qhgk", queries, key_rows, preferred_element_type=jnp.float32)
        * score_scale
    )
    row_count = queries.shape[0]
    causal = (jnp.arange(row_count)[None, :] <= jnp.arange(row_count)[:, None])[:, None, None, :]
    own_top = jnp.max(jnp.where(causal, scores, far_below), axis=-1)
    weights = jnp.where(causal, jnp.exp(scores - own_top[..., None]), 0.0)
    own_total = jnp.sum(weights, axis=-1)
    own_acc = jnp.einsum(
        "qhgk,khd->qhgd",
        weights.astype(jnp.bfloat16),
        value_rows,
        preferred_element_type=jnp.float32,
    )
    return (own_top, own_total, own_acc)


def combine_terms(block_top, block_total, block_acc, own_top, own_total, own_acc):
    row_peak = jnp.maximum(own_top, jnp.max(block_top, axis=0))
    block_scale = jnp.exp(block_top - row_peak)
    own_scale = jnp.exp(own_top - row_peak)
    numerator = own_acc * own_scale[..., None] + jnp.sum(block_acc * block_scale[..., None], axis=0)
    denominator = own_total * own_scale + jnp.sum(block_total * block_scale, axis=0)
    return (numerator / denominator[..., None]).astype(jnp.bfloat16)


def general_body(hidden, gain, w_query, w_key, w_value, w_out, cache, block_slot, retrieved, counts):
    devices = lax.axis_size("dev")
    owner_index = lax.axis_index("dev")
    group_size = HEADS // KV_HEADS
    score_scale = HEAD_DIM ** (-0.5)
    pair_width = KV_HEADS * HEAD_DIM
    query_width = HEADS * HEAD_DIM
    state = hidden[0].astype(jnp.float32)
    inverse = lax.rsqrt(jnp.mean(state * state, axis=-1, keepdims=True) + norm_eps)
    normed = (state * inverse * gain[0]).astype(jnp.bfloat16)
    stacked = jnp.concatenate([w_query[0], w_key[0], w_value[0]], axis=1)
    query_cols = w_query.shape[2]
    key_cols = w_key.shape[2]
    projected = jnp.dot(
        lax.all_gather(normed, "dev", axis=0, tiled=True),
        stacked,
        preferred_element_type=jnp.float32,
    ).astype(jnp.bfloat16)
    query_part = projected[:, :query_cols]
    key_part = projected[:, query_cols : query_cols + key_cols]
    value_part = projected[:, query_cols + key_cols :]
    query_flat, key_flat, value_flat = (
        lax.all_to_all(query_part, "dev", split_axis=0, concat_axis=1, tiled=True),
        lax.all_to_all(key_part, "dev", split_axis=0, concat_axis=1, tiled=True),
        lax.all_to_all(value_part, "dev", split_axis=0, concat_axis=1, tiled=True),
    )
    question = query_flat.shape[0]
    queries = query_flat.reshape(question, KV_HEADS, group_size, HEAD_DIM)
    own_keys = key_flat.reshape(question, KV_HEADS, HEAD_DIM)
    own_values = value_flat.reshape(question, KV_HEADS, HEAD_DIM)
    all_ids, all_counts = (
        lax.all_gather(retrieved[0], "dev", axis=0, tiled=True),
        lax.all_gather(counts[0], "dev", axis=0, tiled=True),
    )
    table_rows = cache.shape[1]
    slot_ids = lookup_slots(all_ids, block_slot)
    listed = jnp.arange(all_ids.shape[1], dtype=jnp.int32)[None, :] < all_counts[:, None]
    mine = listed & (slot_ids // table_rows == owner_index)
    local_row = slot_ids % table_rows
    picked = jnp.sum(
        (
            mine[:, :, None] & (local_row[:, :, None] == jnp.arange(table_rows, dtype=jnp.int32))
        ).astype(jnp.bfloat16),
        axis=1,
    )
    selected = jnp.einsum(
        "rb,btc->rtc", picked, cache[0], preferred_element_type=jnp.float32
    ).astype(jnp.bfloat16)
    own_top, own_total, own_acc = self_stats(queries, own_keys, own_values, score_scale)
    my_slots = lookup_slots(retrieved[0][0], block_slot)
    my_listed = jnp.arange(retrieved.shape[2], dtype=jnp.int32) < counts[0][0]
    owner_ids = jnp.arange(devices, dtype=jnp.int32)
    holders = jnp.any(
        my_listed[None, :] & (my_slots[None, :] // table_rows == owner_ids[:, None]), axis=1
    )
    arrived = lax.all_to_all(selected, "dev", split_axis=0, concat_axis=0, tiled=True)
    arrived_keys = arrived[:, :, :pair_width].reshape(devices, -1, KV_HEADS, HEAD_DIM)
    arrived_values = arrived[:, :, pair_width:].reshape(devices, -1, KV_HEADS, HEAD_DIM)
    scores = (
        jnp.einsum("qhgd,tbhd->tqhgb", queries, arrived_keys, preferred_element_type=jnp.float32)
        * score_scale
    )
    block_top, block_total, weights = block_stats(scores, holders)
    block_acc = jnp.einsum(
        "tqhgb,tbhd->tqhgd", weights, arrived_values, preferred_element_type=jnp.float32
    )
    block_acc = jnp.where(holders[:, None, None, None, None], block_acc, 0.0)
    context = combine_terms(block_top, block_total, block_acc, own_top, own_total, own_acc).reshape(
        question, query_width
    )
    branch_cols = jnp.dot(
        lax.all_gather(context, "dev", axis=0, tiled=True),
        w_out[0],
        preferred_element_type=jnp.float32,
    )
    branch = lax.all_to_all(branch_cols, "dev", split_axis=0, concat_axis=1, tiled=True)
    updated = (state + branch).astype(jnp.bfloat16)
    return passed_along(updated[None], "segment", 1)


CORES = 2
TAIL = 16
LANES = 128
VMEM = pl.BlockSpec(memory_space=pltpu.VMEM)
SMEM = pl.BlockSpec(memory_space=pltpu.SMEM)
ANYWHERE = pl.BlockSpec(memory_space=pl.ANY)
HBM = pl.BlockSpec(memory_space=pltpu.HBM)
MIB = 1 << 20


def to_pair(x, k):
    size = lax.axis_size("dev")
    return lax.ppermute(x, "dev", [(d, d ^ (CORES * k)) for d in range(size)])


def to_partner(x):
    return lax.ppermute(x, "dev", [(d, d ^ 1) for d in range(lax.axis_size("dev"))])


def from_all(x):
    arrived = [x] + [to_pair(x, k) for k in range(1, KV_HEADS)]
    return [p for a in arrived for p in (a, to_partner(a))]


def after(x, *others):
    return lax.optimization_barrier((x, *others))[0]


def in_vmem(x):
    return pltpu.with_memory_space_constraint(x, pltpu.VMEM)


def my_place():
    me = lax.axis_index("dev")
    return me, me // CORES, lax.rem(me, CORES)


def matmul(a, b, dims=((1,), (0,))):
    return lax.dot_general(a, b, (dims, ((), ())), preferred_element_type=jnp.float32)


def load_kernel(count, *refs):
    sources, targets, sems = refs[:count], refs[count : 2 * count], refs[2 * count]
    copies = []
    for i in range(count):
        parts = sems.shape[1]
        depth = targets[i].shape[0] // parts
        for j in range(parts):
            rows = pl.ds(j * depth, depth)
            source = sources[i].at[rows] if len(sources[i].shape) == 2 else sources[i].at[0, rows]
            copies.append(pltpu.make_async_copy(source, targets[i].at[rows], sems.at[i, j]))
    for copy in copies:
        copy.start()
    for copy in copies:
        copy.wait()


def load(*arrays):
    return pl.pallas_call(
        functools.partial(load_kernel, len(arrays)),
        out_shape=[pltpu.VMEM(a.shape[-2:], a.dtype) for a in arrays],
        in_specs=[HBM] * len(arrays),
        out_specs=[VMEM] * len(arrays),
        scratch_shapes=[pltpu.SemaphoreType.DMA((len(arrays), 4))],
        compiler_params=pltpu.CompilerParams(vmem_limit_bytes=2 * MIB),
        cost_estimate=pl.CostEstimate(flops=0, bytes_accessed=0, transcendentals=0),
        name="load",
    )(*[pltpu.with_memory_space_constraint(a, pltpu.HBM) for a in arrays])


def pack_kernel(counts, table_in, retrieved_in, state_in, cache, *rest):
    outs, (whole, state, table, retrieved, sems, list_sems) = rest[:KV_HEADS], rest[KV_HEADS:]
    _, pair, _ = my_place()
    lists = [
        pltpu.make_async_copy(source, target, list_sems.at[i])
        for i, (source, target) in enumerate(
            ((table_in, table), (retrieved_in, retrieved), (state_in, state))
        )
    ]
    lines, tokens = whole.shape[0], whole.shape[1]
    width = whole.shape[2] // 2
    copies = [
        pltpu.make_async_copy(cache.at[0, line], whole.at[line], sems.at[line]) for line in range(lines)
    ]
    for copy in lists + copies:
        copy.start()
    for copy in lists:
        copy.wait()
    listed = retrieved.shape[2]
    lane = lax.broadcasted_iota(jnp.int32, (TAIL, HEAD_DIM), 1)
    note = jnp.where(lane == listed, counts[0, 0], 0)
    for k in range(listed):
        note = jnp.where(lane == k, table[retrieved[0, 0, k]], note)
    note = note.astype(jnp.float32).astype(jnp.bfloat16)
    end = lines * 2 * tokens
    for out in outs:
        out[end : end + TAIL, :] = note
    rows = state.shape[0]
    for t in range(state.shape[1] // LANES // 2):
        tile = jnp.concatenate(
            [
                state[:, i * LANES : (i + 1) * LANES].astype(jnp.float32)
                for i in (2 * t, 2 * t + 1)
            ],
            axis=0,
        ).astype(jnp.bfloat16)
        at = end + TAIL + 2 * rows * t
        for out in outs[:-1]:
            out[at : at + 2 * rows, :] = tile
    for line in range(lines):
        copies[line].wait()
        for k, out in enumerate(outs):
            head = lax.bitwise_xor(pair, k)
            for part in range(2):
                columns = pl.ds(pl.multiple_of(part * width + head * HEAD_DIM, HEAD_DIM), HEAD_DIM)
                at = (line * 2 + part) * tokens
                out[at : at + tokens, :] = whole[line, :, columns]


def pack(table, retrieved, counts, state, cache):
    rows, tokens = cache.shape[1], cache.shape[2]
    short = rows * 2 * tokens + TAIL
    long = short + state.size // HEAD_DIM
    return pl.pallas_call(
        pack_kernel,
        out_shape=[
            pltpu.VMEM((long if k < KV_HEADS - 1 else short, HEAD_DIM), cache.dtype)
            for k in range(KV_HEADS)
        ],
        in_specs=[SMEM] + [HBM] * 4,
        out_specs=[VMEM] * KV_HEADS,
        scratch_shapes=[
            pltpu.VMEM(cache.shape[1:], cache.dtype),
            pltpu.VMEM(state.shape, state.dtype),
            pltpu.SMEM(table.shape, table.dtype),
            pltpu.SMEM(retrieved.shape, retrieved.dtype),
            pltpu.SemaphoreType.DMA((rows,)),
            pltpu.SemaphoreType.DMA((3,)),
        ],
        compiler_params=pltpu.CompilerParams(vmem_limit_bytes=6 * MIB),
        cost_estimate=pl.CostEstimate(flops=0, bytes_accessed=0, transcendentals=0),
        name="pack",
    )(counts, *[pltpu.with_memory_space_constraint(a, pltpu.HBM) for a in (table, retrieved, state, cache)])


def project_kernel(*refs):
    count = 2 * KV_HEADS
    parts, rest = refs[:count], refs[count:]
    gain, wk, wv, normed, kv_out, cols_out = rest
    me, pair, core = my_place()
    first = core == 0
    tiles = gain.shape[0]
    rows = normed.shape[0] // count
    mine = cols_out.shape[1] // LANES
    for k in range(KV_HEADS):
        source = lax.bitwise_xor(pair, k)
        at = pl.ds(pl.multiple_of(source * 2 * rows, 2 * rows), 2 * rows)
        pieces, selected = [], []
        for p in range(CORES):
            part = parts[2 * k + p]
            start = part.shape[0] - tiles * rows
            state = part[start:, :].astype(jnp.float32).reshape(tiles, rows, LANES)
            square = jnp.sum(jnp.sum(state * state, axis=0), axis=-1, keepdims=True)
            inverse = lax.rsqrt(square / (tiles * LANES) + norm_eps)
            pieces.append(state * inverse[None] * gain[...][:, None, :])
            offset = pl.multiple_of(start + me * mine * rows, 2 * rows)
            selected.append(
                part[pl.ds(offset, mine * rows), :].astype(jnp.float32).reshape(mine, rows, LANES)
            )
        low, high = jnp.where(first, *pieces), jnp.where(first, *pieces[::-1])
        for t in range(tiles):
            normed[at, t * LANES : (t + 1) * LANES] = jnp.concatenate([low[t], high[t]], axis=0).astype(
                normed.dtype
            )
        low, high = jnp.where(first, *selected), jnp.where(first, *selected[::-1])
        for t in range(mine):
            cols_out[at, t * LANES : (t + 1) * LANES] = jnp.concatenate(
                [low[t], high[t]], axis=0
            ).astype(cols_out.dtype)
    key = matmul(normed[...], wk[...], ((1,), (1,)))
    value = matmul(normed[...], wv[...], ((1,), (1,)))
    kv_out[...] = jnp.concatenate([key, value], axis=1).astype(kv_out.dtype)


def project(parts, gain, wk, wv, tokens):
    width = wk.shape[1]
    bf16 = jnp.bfloat16
    return pl.pallas_call(
        project_kernel,
        out_shape=[
            pltpu.VMEM((tokens, width), bf16),
            pltpu.VMEM((tokens, 2 * wk.shape[0]), bf16),
            pltpu.VMEM((tokens, width // len(parts)), bf16),
        ],
        in_specs=[VMEM] * (len(parts) + 3),
        out_specs=[VMEM] * 3,
        compiler_params=pltpu.CompilerParams(vmem_limit_bytes=12 * MIB),
        cost_estimate=pl.CostEstimate(flops=0, bytes_accessed=0, transcendentals=0),
        name="project",
    )(*[in_vmem(p) for p in parts], gain.reshape(-1, LANES), in_vmem(wk), in_vmem(wv))


def query_kernel(normed, wq, out):
    out[...] = matmul(normed[...], wq[...]).astype(out.dtype)


def query(normed, wq):
    return pl.pallas_call(
        query_kernel,
        out_shape=pltpu.VMEM((normed.shape[0], wq.shape[1]), jnp.bfloat16),
        in_specs=[VMEM] * 2,
        out_specs=VMEM,
        compiler_params=pltpu.CompilerParams(vmem_limit_bytes=12 * MIB),
        cost_estimate=pl.CostEstimate(
            flops=0, bytes_accessed=0, transcendentals=0
        ),
        name="query",
    )(in_vmem(normed), in_vmem(wq))


def attend_kernel(q, kv_mine, kv_other, *refs):
    count = 2 * KV_HEADS
    held, (out, blocks, placed, scored, notes, tail_vm, meta, sems, note_sems) = refs[:count], refs[count:]
    requests, listed = scored.shape[:2]
    tokens = q.shape[0]
    question = tokens // requests
    heads = q.shape[1] // HEAD_DIM
    group = heads * question
    block = scored.shape[3]
    rows = (blocks.shape[1] - TAIL) // (2 * block)
    me, pair, core = my_place()
    tail, whole = pl.ds(rows * 2 * block, TAIL), pl.ds(0, rows * 2 * block + TAIL)
    tails = [
        pltpu.make_async_copy(held[i].at[tail], tail_vm.at[i], note_sems.at[i]) for i in range(count)
    ]
    copies = [pltpu.make_async_copy(held[i].at[whole], blocks.at[i], sems.at[i]) for i in range(count)]
    for copy in tails + copies:
        copy.start()
    scale = HEAD_DIM ** (-0.5)
    first = core == 0
    half = HEAD_DIM // 2
    a, b = kv_mine[...].astype(jnp.float32), kv_other[...].astype(jnp.float32)
    lo, hi = jnp.where(first, a, b), jnp.where(first, b, a)
    own_key = jnp.concatenate([lo[:, :half], hi[:, :half]], axis=1).astype(jnp.bfloat16)
    own_value = jnp.concatenate([lo[:, half:], hi[:, half:]], axis=1).astype(jnp.bfloat16)
    wide = q[...].astype(jnp.float32)
    queries = []
    for r in range(requests):
        piece = wide[r * question : (r + 1) * question]
        queries.append(
            jnp.concatenate(
                [piece[:, h * HEAD_DIM : (h + 1) * HEAD_DIM] for h in range(heads)], axis=0
            ).astype(jnp.bfloat16)
        )
    stacked = jnp.concatenate(queries, axis=0)
    for copy in tails:
        copy.wait()
    notes[...] = jnp.concatenate(
        [tail_vm[i].astype(jnp.float32)[:1] for i in range(count)], axis=0
    ).astype(jnp.int32)
    noted = pltpu.make_async_copy(notes, meta, note_sems.at[count])
    noted.start()
    scores = matmul(stacked, own_key, ((1,), (1,))) * scale
    row = lax.broadcasted_iota(jnp.int32, scores.shape, 0)
    column = lax.broadcasted_iota(jnp.int32, scores.shape, 1)
    seen = (row // group == column // question) & (column % question <= row % question)
    own_top = jnp.max(jnp.where(seen, scores, far_below), axis=-1, keepdims=True)
    weights = jnp.where(seen, jnp.exp(scores - own_top), 0.0)
    own_total = jnp.sum(weights, axis=-1, keepdims=True)
    own_acc = matmul(weights.astype(jnp.bfloat16), own_value)
    noted.wait()
    for copy in copies:
        copy.wait()
    lives, places = [], []
    for r in range(requests):
        at = lax.bitwise_xor(me, r)
        lives.append(meta[at, listed])
        for k in range(listed):
            slot = meta[at, k]
            source = lax.bitwise_xor(me, slot // rows)
            key_at = pl.multiple_of(lax.rem(slot, rows) * 2 * block, block)
            places.append((source, key_at))
            scored[r, k] = matmul(queries[r], blocks[source, pl.ds(key_at, block), :], ((1,), (1,))) * scale
    scores = scored[...]
    tops = jnp.max(scores, axis=-1, keepdims=True)
    weights = jnp.exp(scores - tops)
    totals = jnp.sum(weights, axis=-1, keepdims=True)
    scored[...] = weights
    for r in range(requests):
        mine = slice(r * group, (r + 1) * group)
        live = lives[r]
        accs, marks = [], []
        for k in range(listed):
            source, key_at = places[r * listed + k]
            values = blocks[source, pl.ds(key_at + block, block), :]
            accs.append(matmul(scored[r, k].astype(jnp.bfloat16), values))
            marks.append(jnp.where(k < live, tops[r, k], far_below))
        peak = own_top[mine]
        for mark in marks:
            peak = jnp.maximum(peak, mark)
        factor = jnp.exp(own_top[mine] - peak)
        numerator, denominator = own_acc[mine] * factor, own_total[mine] * factor
        for k in range(listed):
            factor = jnp.where(k < live, jnp.exp(marks[k] - peak), 0.0)
            numerator = numerator + accs[k] * factor
            denominator = denominator + totals[r, k] * factor
        context = numerator / denominator
        for h in range(heads):
            placed[r * question : (r + 1) * question, h * HEAD_DIM : (h + 1) * HEAD_DIM] = context[
                h * question : (h + 1) * question
            ]
    out[...] = placed[...].astype(out.dtype)


def attend(q, kv_mine, kv_other, held, requests, listed, block):
    count = len(held)
    return pl.pallas_call(
        attend_kernel,
        out_shape=pltpu.VMEM(q.shape, jnp.bfloat16),
        in_specs=[VMEM] * 3 + [ANYWHERE] * count,
        out_specs=VMEM,
        scratch_shapes=[
            pltpu.VMEM((count, *held[-1].shape), jnp.bfloat16),
            pltpu.VMEM(q.shape, jnp.float32),
            pltpu.VMEM((requests, listed, q.size // HEAD_DIM // requests, block), jnp.float32),
            pltpu.VMEM((count, HEAD_DIM), jnp.int32),
            pltpu.VMEM((count, TAIL, HEAD_DIM), jnp.bfloat16),
            pltpu.SMEM((count, HEAD_DIM), jnp.int32),
            pltpu.SemaphoreType.DMA((count,)),
            pltpu.SemaphoreType.DMA((count + 1,)),
        ],
        compiler_params=pltpu.CompilerParams(vmem_limit_bytes=16 * MIB),
        cost_estimate=pl.CostEstimate(
            flops=1 << 28, bytes_accessed=2 * MIB, transcendentals=1 << 18
        ),
        name="attend",
    )(in_vmem(q), in_vmem(kv_mine), in_vmem(kv_other), *held)


def partial_kernel(*refs):
    parts, (w_out, out) = refs[:-2], refs[-2:]
    me, _, _ = my_place()
    depth = parts[0].shape[1]
    total = None
    for i, part in enumerate(parts):
        source = lax.bitwise_xor(me, i)
        span = pl.ds(pl.multiple_of(source * depth, depth), depth)
        product = matmul(part[...], w_out[span, :])
        total = product if total is None else total + product
    out[...] = total


def partial_branch(parts, w_out):
    tokens, width = parts[0].shape[0], w_out.shape[1]
    return pl.pallas_call(
        partial_kernel,
        out_shape=pltpu.VMEM((tokens, width), jnp.float32),
        in_specs=[VMEM] * (len(parts) + 1),
        out_specs=VMEM,
        compiler_params=pltpu.CompilerParams(vmem_limit_bytes=12 * MIB),
        cost_estimate=pl.CostEstimate(
            flops=tokens * w_out.size, bytes_accessed=w_out.size, transcendentals=0
        ),
        name="partial",
    )(*[in_vmem(p) for p in parts], in_vmem(w_out))


def finish_kernel(*refs):
    outs, placed = refs[-1 - KV_HEADS : -1], refs[-1]
    parts, (before, cols, w_out) = refs[: -4 - KV_HEADS], refs[-4 - KV_HEADS : -1 - KV_HEADS]
    me, pair, _ = my_place()
    depth = parts[0].shape[1]
    total = before[...]
    for i, part in enumerate(parts):
        source = lax.bitwise_xor(me, 2 * KV_HEADS - len(parts) + i)
        span = pl.ds(pl.multiple_of(source * depth, depth), depth)
        total = total + matmul(part[...], w_out[span, :])
    placed[...] = cols[...].astype(jnp.float32) + total
    rows = outs[0].shape[0]
    for k, out in enumerate(outs):
        target = lax.bitwise_xor(pair, k)
        out[...] = placed[pl.ds(pl.multiple_of(target * rows, rows), rows), :].astype(out.dtype)


def finish(parts, before, cols, w_out):
    tokens, width = cols.shape
    shape = pltpu.VMEM((tokens // KV_HEADS, width), jnp.bfloat16)
    return pl.pallas_call(
        finish_kernel,
        out_shape=[shape] * KV_HEADS,
        in_specs=[VMEM] * (len(parts) + 3),
        out_specs=[VMEM] * KV_HEADS,
        scratch_shapes=[pltpu.VMEM((tokens, width), jnp.float32)],
        compiler_params=pltpu.CompilerParams(vmem_limit_bytes=12 * MIB),
        cost_estimate=pl.CostEstimate(
            flops=tokens * w_out.size, bytes_accessed=w_out.size, transcendentals=0
        ),
        name="finish",
    )(*[in_vmem(p) for p in parts], in_vmem(before), in_vmem(cols), in_vmem(w_out))


def place_kernel(order, *refs):
    parts, out = refs[:-1], refs[-1]
    me, _, core = my_place()
    rows, width = out.shape[1], parts[0].shape[1]
    for i, part in zip(order, parts, strict=True):
        source = lax.bitwise_xor(me, i)
        both = part[...].astype(jnp.float32)
        mine = jnp.where(core == 0, both[:rows], both[rows:])
        out[0, :, pl.ds(pl.multiple_of(source * width, width), width)] = mine.astype(out.dtype)


def place_columns(parts):
    order = sorted(parts, reverse=True)
    rows, width = parts[0].shape
    return pl.pallas_call(
        functools.partial(place_kernel, order),
        out_shape=jax.ShapeDtypeStruct((1, rows // CORES, width * len(parts)), jnp.bfloat16),
        in_specs=[VMEM] * len(parts),
        out_specs=VMEM,
        compiler_params=pltpu.CompilerParams(vmem_limit_bytes=4 * MIB),
        name="place",
    )(*[in_vmem(parts[i]) for i in order])


def by_head(hidden, gain, w_query, w_key, w_value, w_out, cache, block_slot, retrieved, counts):
    size, sections = lax.axis_size("dev"), lax.axis_size("segment")
    packed = pack(block_slot, retrieved, counts, hidden[0], cache)
    weights = load(w_query, w_key[0].swapaxes(0, 1), w_value[0].swapaxes(0, 1))
    second, first, far = to_pair(packed[2], 2), to_pair(packed[1], 1), to_pair(packed[3], 3)
    second, weights = lax.optimization_barrier((second, weights))
    crossed = to_pair(second[packed[3].shape[0] :], 1)
    held = [h for a in (packed[0], first, second) for h in (a, to_partner(a))]
    held, crossed, (wq, wk, wv) = lax.optimization_barrier((held, crossed, weights))
    parts = [*held, crossed, to_partner(crossed)]
    tokens = size * hidden.shape[1]
    normed, kv, cols = project(parts, gain, wk, wv, tokens)
    kv_other = to_partner(kv)
    q = query(normed, wq)
    far, q, kv_other = lax.optimization_barrier((far, q, kv_other))
    held += [far, to_partner(far)]
    context = attend(q, kv, kv_other, held, size, retrieved.shape[2], cache.shape[2])
    contexts = {0: context, 2: to_pair(context, 2), 1: to_pair(context, 1)}
    contexts[3] = to_pair(contexts[2], 1)
    contexts = [p for k in range(KV_HEADS) for p in (contexts[k], to_partner(contexts[k]))]
    before = partial_branch(contexts[:4], w_out[0])
    pieces = finish(contexts[4:], before, cols, w_out[0])
    final = {}
    for k in (3, 2, 1, 0):
        route = [
            (s * size + d, (s + 1) % sections * size + (d ^ (CORES * k)))
            for s in range(sections)
            for d in range(size)
        ]
        final[2 * k] = lax.ppermute(pieces[k], ("segment", "dev"), route)
        final[2 * k + 1] = to_partner(final[2 * k])
    return place_columns(final)


def solution(mesh):
    heads_fit = mesh.shape["dev"] == CORES * KV_HEADS
    return jax.shard_map(
        by_head if heads_fit else general_body,
        mesh=mesh,
        in_specs=(
            P("segment", "dev", None),
            P("segment", None),
            P("segment", None, "dev"),
            P("segment", None, "dev"),
            P("segment", None, "dev"),
            P("segment", None, "dev"),
            P("segment", "dev", None, None),
            P(),
            P("segment", "dev", None),
            P("segment", "dev"),
        ),
        out_specs=P("segment", "dev", None),
        check_vma=False,
    )
```

```python
import functools

import jax
import jax.numpy as jnp
from jax import lax
from jax.experimental import pallas as pl
from jax.experimental.pallas import tpu as pltpu
from jax.sharding import PartitionSpec as P

HEADS = 32
KV_HEADS = 4
HEAD_DIM = 128


far_below = -1e30
norm_eps = 1e-05


def passed_along(shard, axis, by):
    size = lax.axis_size(axis)
    return lax.ppermute(shard, axis, [(i, (i + by) % size) for i in range(size)])


def lookup_slots(block_ids, block_slot):
    table_width = block_slot.shape[0]
    matches = block_ids[..., None] == jnp.arange(table_width, dtype=jnp.int32)
    return jnp.sum(jnp.where(matches, block_slot, 0), axis=-1)


def block_stats(scores, valid):
    block_top = jnp.max(scores, axis=-1)
    weights = jnp.exp(scores - block_top[..., None])
    block_total = jnp.sum(weights, axis=-1)
    live_mask = valid[:, None, None, None]
    block_top = jnp.where(live_mask, block_top, far_below)
    block_total = jnp.where(live_mask, block_total, 0.0)
    return (block_top, block_total, weights.astype(jnp.bfloat16))


def self_stats(queries, key_rows, value_rows, score_scale):
    scores = (
        jnp.einsum("qhgd,khd->qhgk", queries, key_rows, preferred_element_type=jnp.float32)
        * score_scale
    )
    row_count = queries.shape[0]
    causal = (jnp.arange(row_count)[None, :] <= jnp.arange(row_count)[:, None])[:, None, None, :]
    own_top = jnp.max(jnp.where(causal, scores, far_below), axis=-1)
    weights = jnp.where(causal, jnp.exp(scores - own_top[..., None]), 0.0)
    own_total = jnp.sum(weights, axis=-1)
    own_acc = jnp.einsum(
        "qhgk,khd->qhgd",
        weights.astype(jnp.bfloat16),
        value_rows,
        preferred_element_type=jnp.float32,
    )
    return (own_top, own_total, own_acc)


def combine_terms(block_top, block_total, block_acc, own_top, own_total, own_acc):
    row_peak = jnp.maximum(own_top, jnp.max(block_top, axis=0))
    block_scale = jnp.exp(block_top - row_peak)
    own_scale = jnp.exp(own_top - row_peak)
    numerator = own_acc * own_scale[..., None] + jnp.sum(block_acc * block_scale[..., None], axis=0)
    denominator = own_total * own_scale + jnp.sum(block_total * block_scale, axis=0)
    return (numerator / denominator[..., None]).astype(jnp.bfloat16)


def general_body(hidden, gain, w_query, w_key, w_value, w_out, cache, block_slot, retrieved, counts):
    devices = lax.axis_size("dev")
    owner_index = lax.axis_index("dev")
    group_size = HEADS // KV_HEADS
    score_scale = HEAD_DIM ** (-0.5)
    pair_width = KV_HEADS * HEAD_DIM
    query_width = HEADS * HEAD_DIM
    state = hidden[0].astype(jnp.float32)
    inverse = lax.rsqrt(jnp.mean(state * state, axis=-1, keepdims=True) + norm_eps)
    normed = (state * inverse * gain[0]).astype(jnp.bfloat16)
    stacked = jnp.concatenate([w_query[0], w_key[0], w_value[0]], axis=1)
    query_cols = w_query.shape[2]
    key_cols = w_key.shape[2]
    projected = jnp.dot(
        lax.all_gather(normed, "dev", axis=0, tiled=True),
        stacked,
        preferred_element_type=jnp.float32,
    ).astype(jnp.bfloat16)
    query_part = projected[:, :query_cols]
    key_part = projected[:, query_cols : query_cols + key_cols]
    value_part = projected[:, query_cols + key_cols :]
    query_flat, key_flat, value_flat = (
        lax.all_to_all(query_part, "dev", split_axis=0, concat_axis=1, tiled=True),
        lax.all_to_all(key_part, "dev", split_axis=0, concat_axis=1, tiled=True),
        lax.all_to_all(value_part, "dev", split_axis=0, concat_axis=1, tiled=True),
    )
    question = query_flat.shape[0]
    queries = query_flat.reshape(question, KV_HEADS, group_size, HEAD_DIM)
    own_keys = key_flat.reshape(question, KV_HEADS, HEAD_DIM)
    own_values = value_flat.reshape(question, KV_HEADS, HEAD_DIM)
    all_ids, all_counts = (
        lax.all_gather(retrieved[0], "dev", axis=0, tiled=True),
        lax.all_gather(counts[0], "dev", axis=0, tiled=True),
    )
    table_rows = cache.shape[1]
    slot_ids = lookup_slots(all_ids, block_slot)
    listed = jnp.arange(all_ids.shape[1], dtype=jnp.int32)[None, :] < all_counts[:, None]
    mine = listed & (slot_ids // table_rows == owner_index)
    local_row = slot_ids % table_rows
    picked = jnp.sum(
        (
            mine[:, :, None] & (local_row[:, :, None] == jnp.arange(table_rows, dtype=jnp.int32))
        ).astype(jnp.bfloat16),
        axis=1,
    )
    selected = jnp.einsum(
        "rb,btc->rtc", picked, cache[0], preferred_element_type=jnp.float32
    ).astype(jnp.bfloat16)
    own_top, own_total, own_acc = self_stats(queries, own_keys, own_values, score_scale)
    my_slots = lookup_slots(retrieved[0][0], block_slot)
    my_listed = jnp.arange(retrieved.shape[2], dtype=jnp.int32) < counts[0][0]
    owner_ids = jnp.arange(devices, dtype=jnp.int32)
    holders = jnp.any(
        my_listed[None, :] & (my_slots[None, :] // table_rows == owner_ids[:, None]), axis=1
    )
    arrived = lax.all_to_all(selected, "dev", split_axis=0, concat_axis=0, tiled=True)
    arrived_keys = arrived[:, :, :pair_width].reshape(devices, -1, KV_HEADS, HEAD_DIM)
    arrived_values = arrived[:, :, pair_width:].reshape(devices, -1, KV_HEADS, HEAD_DIM)
    scores = (
        jnp.einsum("qhgd,tbhd->tqhgb", queries, arrived_keys, preferred_element_type=jnp.float32)
        * score_scale
    )
    block_top, block_total, weights = block_stats(scores, holders)
    block_acc = jnp.einsum(
        "tqhgb,tbhd->tqhgd", weights, arrived_values, preferred_element_type=jnp.float32
    )
    block_acc = jnp.where(holders[:, None, None, None, None], block_acc, 0.0)
    context = combine_terms(block_top, block_total, block_acc, own_top, own_total, own_acc).reshape(
        question, query_width
    )
    branch_cols = jnp.dot(
        lax.all_gather(context, "dev", axis=0, tiled=True),
        w_out[0],
        preferred_element_type=jnp.float32,
    )
    branch = lax.all_to_all(branch_cols, "dev", split_axis=0, concat_axis=1, tiled=True)
    updated = (state + branch).astype(jnp.bfloat16)
    return passed_along(updated[None], "segment", 1)


CORES = 2
TAIL = 16
VMEM = pl.BlockSpec(memory_space=pltpu.VMEM)
SMEM = pl.BlockSpec(memory_space=pltpu.SMEM)
ANYWHERE = pl.BlockSpec(memory_space=pl.ANY)
HBM = pl.BlockSpec(memory_space=pltpu.HBM)
MIB = 1 << 20


def to_pair(x, k):
    size = lax.axis_size("dev")
    return lax.ppermute(x, "dev", [(d, d ^ (CORES * k)) for d in range(size)])


def to_partner(x):
    return lax.ppermute(x, "dev", [(d, d ^ 1) for d in range(lax.axis_size("dev"))])


def from_all(x):
    arrived = [x] + [to_pair(x, k) for k in range(1, KV_HEADS)]
    return [p for a in arrived for p in (a, to_partner(a))]


def after(x, *others):
    return lax.optimization_barrier((x, *others))[0]


def in_vmem(x):
    return pltpu.with_memory_space_constraint(x, pltpu.VMEM)


def my_place():
    me = lax.axis_index("dev")
    return me, me // CORES, lax.rem(me, CORES)


def matmul(a, b, dims=((1,), (0,))):
    return lax.dot_general(a, b, (dims, ((), ())), preferred_element_type=jnp.float32)


def load_kernel(count, *refs):
    sources, targets, sems = refs[:count], refs[count : 2 * count], refs[2 * count]
    copies = []
    for i in range(count):
        parts = sems.shape[1]
        depth = targets[i].shape[0] // parts
        for j in range(parts):
            rows = pl.ds(j * depth, depth)
            source = sources[i].at[rows] if len(sources[i].shape) == 2 else sources[i].at[0, rows]
            copies.append(pltpu.make_async_copy(source, targets[i].at[rows], sems.at[i, j]))
    for copy in copies:
        copy.start()
    for copy in copies:
        copy.wait()


def load(*arrays):
    return pl.pallas_call(
        functools.partial(load_kernel, len(arrays)),
        out_shape=[pltpu.VMEM(a.shape[-2:], a.dtype) for a in arrays],
        in_specs=[HBM] * len(arrays),
        out_specs=[VMEM] * len(arrays),
        scratch_shapes=[pltpu.SemaphoreType.DMA((len(arrays), 4))],
        compiler_params=pltpu.CompilerParams(vmem_limit_bytes=2 * MIB),
        cost_estimate=pl.CostEstimate(flops=0, bytes_accessed=0, transcendentals=0),
        name="load",
    )(*[pltpu.with_memory_space_constraint(a, pltpu.HBM) for a in arrays])


def pack_kernel(counts, table_in, retrieved_in, cache, *rest):
    outs, (whole, table, retrieved, sems, list_sems) = rest[:-5], rest[-5:]
    lists = [
        pltpu.make_async_copy(source, target, list_sems.at[i])
        for i, (source, target) in enumerate(
            ((table_in, table), (retrieved_in, retrieved))
        )
    ]
    for copy in lists:
        copy.start()
    lines, tokens = whole.shape[0], whole.shape[1]
    width = whole.shape[2] // 2
    copies = [
        pltpu.make_async_copy(cache.at[0, line], whole.at[line], sems.at[line]) for line in range(lines)
    ]
    for copy in copies:
        copy.start()
    for copy in lists:
        copy.wait()
    listed = retrieved.shape[2]
    lane = lax.broadcasted_iota(jnp.int32, (TAIL, HEAD_DIM), 1)
    note = jnp.where(lane == listed, counts[0, 0], 0)
    for k in range(listed):
        note = jnp.where(lane == k, table[retrieved[0, 0, k]], note)
    note = note.astype(jnp.float32).astype(jnp.bfloat16)
    for out in outs:
        out[lines * 2 * tokens :, :] = note
    for line in range(lines):
        copies[line].wait()
        for k, out in enumerate(outs):
            head = lax.bitwise_xor(my_place()[1], k)
            for part in range(2):
                columns = pl.ds(pl.multiple_of(part * width + head * HEAD_DIM, HEAD_DIM), HEAD_DIM)
                at = (line * 2 + part) * tokens
                out[at : at + tokens, :] = whole[line, :, columns]


def pack(table, retrieved, counts, cache):
    rows, tokens = cache.shape[1], cache.shape[2]
    return pl.pallas_call(
        pack_kernel,
        out_shape=[pltpu.VMEM((rows * 2 * tokens + TAIL, HEAD_DIM), cache.dtype)] * KV_HEADS,
        in_specs=[SMEM] + [HBM] * 3,
        out_specs=[VMEM] * KV_HEADS,
        scratch_shapes=[
            pltpu.VMEM(cache.shape[1:], cache.dtype),
            pltpu.SMEM(table.shape, table.dtype),
            pltpu.SMEM(retrieved.shape, retrieved.dtype),
            pltpu.SemaphoreType.DMA((rows,)),
            pltpu.SemaphoreType.DMA((2,)),
        ],
        compiler_params=pltpu.CompilerParams(vmem_limit_bytes=6 * MIB),
        cost_estimate=pl.CostEstimate(flops=0, bytes_accessed=0, transcendentals=0),
        name="pack",
    )(counts, *[pltpu.with_memory_space_constraint(a, pltpu.HBM) for a in (table, retrieved, cache)])


def project_kernel(*refs):
    count = 2 * KV_HEADS
    parts, rest = refs[:count], refs[count:]
    gain, wk, wv, normed, kv_out, cols_out = rest
    _, pair, core = my_place()
    first = core == 0
    width = cols_out.shape[1]
    columns = pl.ds(pl.multiple_of((CORES * pair + core) * width, 128), width)
    for k in range(KV_HEADS):
        source = lax.bitwise_xor(pair, k)
        rows = pl.ds(pl.multiple_of(source * 16, 16), 16)

        def both(at):
            a, b = (parts[2 * k + p][:, at].astype(jnp.float32) for p in range(CORES))
            return jnp.concatenate([jnp.where(first, a, b), jnp.where(first, b, a)], axis=0)

        state = both(slice(None))
        inverse = lax.rsqrt(jnp.mean(state * state, axis=-1, keepdims=True) + norm_eps)
        normed[rows, :] = (state * inverse * gain[...]).astype(jnp.bfloat16)
        cols_out[rows, :] = both(columns).astype(cols_out.dtype)
    key = matmul(normed[...], wk[...], ((1,), (1,)))
    value = matmul(normed[...], wv[...], ((1,), (1,)))
    kv_out[...] = jnp.concatenate([key, value], axis=1).astype(kv_out.dtype)


def project(parts, gain, wk, wv):
    tokens = sum(p.shape[0] for p in parts)
    width = parts[0].shape[1]
    bf16 = jnp.bfloat16
    return pl.pallas_call(
        project_kernel,
        out_shape=[
            pltpu.VMEM((tokens, width), bf16),
            pltpu.VMEM((tokens, 2 * wk.shape[0]), bf16),
            pltpu.VMEM((tokens, width // len(parts)), bf16),
        ],
        in_specs=[VMEM] * (len(parts) + 3),
        out_specs=[VMEM] * 3,
        compiler_params=pltpu.CompilerParams(vmem_limit_bytes=12 * MIB),
        cost_estimate=pl.CostEstimate(
            flops=0, bytes_accessed=0, transcendentals=0
        ),
        name="project",
    )(*[in_vmem(p) for p in parts], gain, in_vmem(wk), in_vmem(wv))


def query_kernel(normed, wq, out):
    out[...] = matmul(normed[...], wq[...]).astype(out.dtype)


def query(normed, wq):
    return pl.pallas_call(
        query_kernel,
        out_shape=pltpu.VMEM((normed.shape[0], wq.shape[1]), jnp.bfloat16),
        in_specs=[VMEM] * 2,
        out_specs=VMEM,
        compiler_params=pltpu.CompilerParams(vmem_limit_bytes=12 * MIB),
        cost_estimate=pl.CostEstimate(
            flops=0, bytes_accessed=0, transcendentals=0
        ),
        name="query",
    )(in_vmem(normed), in_vmem(wq))


def attend_kernel(q, kv_mine, kv_other, *refs):
    count = 2 * KV_HEADS
    held, (out, blocks, placed, scored, notes, tail_vm, meta, sems, note_sems) = refs[:count], refs[count:]
    requests, listed = scored.shape[:2]
    tokens = q.shape[0]
    question = tokens // requests
    heads = q.shape[1] // HEAD_DIM
    group = heads * question
    block = scored.shape[3]
    rows = (blocks.shape[1] - TAIL) // (2 * block)
    me, pair, core = my_place()
    tail = pl.ds(rows * 2 * block, TAIL)
    tails = [
        pltpu.make_async_copy(held[i].at[tail], tail_vm.at[i], note_sems.at[i]) for i in range(count)
    ]
    copies = [pltpu.make_async_copy(held[i], blocks.at[i], sems.at[i]) for i in range(count)]
    for copy in tails + copies:
        copy.start()
    scale = HEAD_DIM ** (-0.5)
    first = core == 0
    half = HEAD_DIM // 2
    a, b = kv_mine[...].astype(jnp.float32), kv_other[...].astype(jnp.float32)
    lo, hi = jnp.where(first, a, b), jnp.where(first, b, a)
    own_key = jnp.concatenate([lo[:, :half], hi[:, :half]], axis=1).astype(jnp.bfloat16)
    own_value = jnp.concatenate([lo[:, half:], hi[:, half:]], axis=1).astype(jnp.bfloat16)
    wide = q[...].astype(jnp.float32)
    queries = []
    for r in range(requests):
        piece = wide[r * question : (r + 1) * question]
        queries.append(
            jnp.concatenate(
                [piece[:, h * HEAD_DIM : (h + 1) * HEAD_DIM] for h in range(heads)], axis=0
            ).astype(jnp.bfloat16)
        )
    stacked = jnp.concatenate(queries, axis=0)
    for copy in tails:
        copy.wait()
    notes[...] = jnp.concatenate(
        [tail_vm[i].astype(jnp.float32)[:1] for i in range(count)], axis=0
    ).astype(jnp.int32)
    noted = pltpu.make_async_copy(notes, meta, note_sems.at[count])
    noted.start()
    scores = matmul(stacked, own_key, ((1,), (1,))) * scale
    row = lax.broadcasted_iota(jnp.int32, scores.shape, 0)
    column = lax.broadcasted_iota(jnp.int32, scores.shape, 1)
    seen = (row // group == column // question) & (column % question <= row % question)
    own_top = jnp.max(jnp.where(seen, scores, far_below), axis=-1, keepdims=True)
    weights = jnp.where(seen, jnp.exp(scores - own_top), 0.0)
    own_total = jnp.sum(weights, axis=-1, keepdims=True)
    own_acc = matmul(weights.astype(jnp.bfloat16), own_value)
    noted.wait()
    for copy in copies:
        copy.wait()
    lives, places = [], []
    for r in range(requests):
        at = lax.bitwise_xor(me, r)
        lives.append(meta[at, listed])
        for k in range(listed):
            slot = meta[at, k]
            source = lax.bitwise_xor(me, slot // rows)
            key_at = pl.multiple_of(lax.rem(slot, rows) * 2 * block, block)
            places.append((source, key_at))
            scored[r, k] = matmul(queries[r], blocks[source, pl.ds(key_at, block), :], ((1,), (1,))) * scale
    scores = scored[...]
    tops = jnp.max(scores, axis=-1, keepdims=True)
    weights = jnp.exp(scores - tops)
    totals = jnp.sum(weights, axis=-1, keepdims=True)
    scored[...] = weights
    for r in range(requests):
        mine = slice(r * group, (r + 1) * group)
        live = lives[r]
        accs, marks = [], []
        for k in range(listed):
            source, key_at = places[r * listed + k]
            values = blocks[source, pl.ds(key_at + block, block), :]
            accs.append(matmul(scored[r, k].astype(jnp.bfloat16), values))
            marks.append(jnp.where(k < live, tops[r, k], far_below))
        peak = own_top[mine]
        for mark in marks:
            peak = jnp.maximum(peak, mark)
        factor = jnp.exp(own_top[mine] - peak)
        numerator, denominator = own_acc[mine] * factor, own_total[mine] * factor
        for k in range(listed):
            factor = jnp.where(k < live, jnp.exp(marks[k] - peak), 0.0)
            numerator = numerator + accs[k] * factor
            denominator = denominator + totals[r, k] * factor
        context = numerator / denominator
        for h in range(heads):
            placed[r * question : (r + 1) * question, h * HEAD_DIM : (h + 1) * HEAD_DIM] = context[
                h * question : (h + 1) * question
            ]
    out[...] = placed[...].astype(out.dtype)


def attend(q, kv_mine, kv_other, held, requests, listed, block):
    count = len(held)
    return pl.pallas_call(
        attend_kernel,
        out_shape=pltpu.VMEM(q.shape, jnp.bfloat16),
        in_specs=[VMEM] * 3 + [ANYWHERE] * count,
        out_specs=VMEM,
        scratch_shapes=[
            pltpu.VMEM((count, *held[0].shape), jnp.bfloat16),
            pltpu.VMEM(q.shape, jnp.float32),
            pltpu.VMEM((requests, listed, q.size // HEAD_DIM // requests, block), jnp.float32),
            pltpu.VMEM((count, HEAD_DIM), jnp.int32),
            pltpu.VMEM((count, TAIL, HEAD_DIM), jnp.bfloat16),
            pltpu.SMEM((count, HEAD_DIM), jnp.int32),
            pltpu.SemaphoreType.DMA((count,)),
            pltpu.SemaphoreType.DMA((count + 1,)),
        ],
        compiler_params=pltpu.CompilerParams(vmem_limit_bytes=16 * MIB),
        cost_estimate=pl.CostEstimate(
            flops=1 << 28, bytes_accessed=2 * MIB, transcendentals=1 << 18
        ),
        name="attend",
    )(in_vmem(q), in_vmem(kv_mine), in_vmem(kv_other), *held)


def partial_kernel(*refs):
    parts, (w_out, out) = refs[:-2], refs[-2:]
    me, _, _ = my_place()
    depth = parts[0].shape[1]
    total = None
    for i, part in enumerate(parts):
        source = lax.bitwise_xor(me, i)
        span = pl.ds(pl.multiple_of(source * depth, depth), depth)
        product = matmul(part[...], w_out[span, :])
        total = product if total is None else total + product
    out[...] = total


def partial_branch(parts, w_out):
    tokens, width = parts[0].shape[0], w_out.shape[1]
    return pl.pallas_call(
        partial_kernel,
        out_shape=pltpu.VMEM((tokens, width), jnp.float32),
        in_specs=[VMEM] * (len(parts) + 1),
        out_specs=VMEM,
        compiler_params=pltpu.CompilerParams(vmem_limit_bytes=12 * MIB),
        cost_estimate=pl.CostEstimate(
            flops=tokens * w_out.size, bytes_accessed=w_out.size, transcendentals=0
        ),
        name="partial",
    )(*[in_vmem(p) for p in parts], in_vmem(w_out))


def away(turn, core):
    return lax.bitwise_xor(3 * (1 - turn), core)


def finish_kernel(*refs):
    parts, (before, cols, w_out, *outs, placed) = refs[:-6], refs[-6:]
    me, pair, core = my_place()
    depth = parts[0].shape[1]
    total = before[...]
    for i, part in enumerate(parts):
        source = lax.bitwise_xor(me, 2 * KV_HEADS - len(parts) + i)
        span = pl.ds(pl.multiple_of(source * depth, depth), depth)
        total = total + matmul(part[...], w_out[span, :])
    placed[...] = cols[...].astype(jnp.float32) + total
    keep, give = outs
    rows = keep.shape[0] // 2
    for k in range(KV_HEADS):
        target = lax.bitwise_xor(pair, away(k % 2, lax.bitwise_xor(core, k // 2)))
        piece = placed[pl.ds(pl.multiple_of(target * rows, rows), rows), :]
        out = (keep, give)[k // 2]
        out[k % 2 * rows : (k % 2 + 1) * rows, :] = piece.astype(out.dtype)


def finish(parts, before, cols, w_out):
    tokens, width = cols.shape
    shape = pltpu.VMEM((tokens // 2, width), jnp.bfloat16)
    return pl.pallas_call(
        finish_kernel,
        out_shape=[shape] * 2,
        in_specs=[VMEM] * (len(parts) + 3),
        out_specs=[VMEM] * 2,
        scratch_shapes=[pltpu.VMEM((tokens, width), jnp.float32)],
        compiler_params=pltpu.CompilerParams(vmem_limit_bytes=12 * MIB),
        cost_estimate=pl.CostEstimate(
            flops=tokens * w_out.size, bytes_accessed=w_out.size, transcendentals=0
        ),
        name="finish",
    )(*[in_vmem(p) for p in parts], in_vmem(before), in_vmem(cols), in_vmem(w_out))


def join_kernel(keep, got, *outs):
    rows = keep.shape[0] // 2
    for k, out in enumerate(outs):
        out[0] = keep[k * rows : (k + 1) * rows, :]
        out[1] = got[k * rows : (k + 1) * rows, :]


def join(keep, got):
    rows, width = keep.shape
    return pl.pallas_call(
        join_kernel,
        out_shape=[pltpu.VMEM((CORES, rows // 2, width), keep.dtype)] * 2,
        in_specs=[VMEM] * 2,
        out_specs=[VMEM] * 2,
        compiler_params=pltpu.CompilerParams(vmem_limit_bytes=4 * MIB),
        name="join",
    )(in_vmem(keep), in_vmem(got))


def place_kernel(*refs):
    parts, out = refs[:-1], refs[-1]
    me, _, core = my_place()
    rows, width = out.shape[1], parts[0].shape[2]
    for i, part in enumerate(parts):
        taker = lax.bitwise_xor(core, i % 2)
        sender = lax.bitwise_xor(me - core + taker, CORES * away(i // 2, taker))
        for p in range(CORES):
            source = lax.bitwise_xor(sender, p)
            both = part[p].astype(jnp.float32)
            mine = jnp.where(core == 0, both[:rows], both[rows:])
            out[0, :, pl.ds(pl.multiple_of(source * width, width), width)] = mine.astype(out.dtype)


def place_columns(parts):
    cores, rows, width = parts[0].shape
    return pl.pallas_call(
        place_kernel,
        out_shape=jax.ShapeDtypeStruct((1, rows // CORES, width * cores * len(parts)), jnp.bfloat16),
        in_specs=[VMEM] * len(parts),
        out_specs=VMEM,
        compiler_params=pltpu.CompilerParams(vmem_limit_bytes=4 * MIB),
        name="place",
    )(*[in_vmem(part) for part in parts])


def by_head(hidden, gain, w_query, w_key, w_value, w_out, cache, block_slot, retrieved, counts):
    size, sections = lax.axis_size("dev"), lax.axis_size("segment")
    state = hidden[0]
    gathered = {2: to_pair(state, 2), 1: to_pair(state, 1)}
    packed = pack(block_slot, retrieved, counts, cache)
    weights = load(w_query, w_key[0].swapaxes(0, 1), w_value[0].swapaxes(0, 1))
    blocks = {k: to_pair(packed[k], k) for k in (3, 2)}
    gathered[2], packed = lax.optimization_barrier((gathered[2], packed))
    gathered[3] = to_pair(gathered[2], 1)
    near, gathered[1] = lax.optimization_barrier((packed[1], gathered[1]))
    blocks[1] = to_pair(near, 1)
    mine, gathered, weights = lax.optimization_barrier((state, gathered, weights))
    wq, wk, wv = weights
    parts = [p for a in (mine, *(gathered[k] for k in (1, 2, 3))) for p in (a, to_partner(a))]
    normed, kv, cols = project(parts, gain, wk, wv)
    kv_other = to_partner(kv)
    q = query(normed, wq)
    own, blocks, q = lax.optimization_barrier((packed[0], blocks, q))
    blocks[0] = own
    held = [h for k in range(KV_HEADS) for h in (blocks[k], to_partner(blocks[k]))]
    context = attend(q, kv, kv_other, held, size, retrieved.shape[2], cache.shape[2])
    contexts = {0: context, 2: to_pair(context, 2), 1: to_pair(context, 1)}
    contexts[3] = to_pair(contexts[2], 1)
    contexts = [p for k in range(KV_HEADS) for p in (contexts[k], to_partner(contexts[k]))]
    before = partial_branch(contexts[:4], w_out[0])
    keep, give = finish(contexts[4:], before, cols, w_out[0])
    final = []
    for k, piece in enumerate(join(keep, to_partner(give))):
        route = [
            (s * size + d, (s + 1) % sections * size + (d ^ (CORES * (3 * (1 - k) ^ d % CORES))))
            for s in range(sections)
            for d in range(size)
        ]
        piece = lax.ppermute(piece, ("segment", "dev"), route)
        final += [piece, to_partner(piece)]
    return place_columns(final)


def solution(mesh):
    heads_fit = mesh.shape["dev"] == CORES * KV_HEADS
    return jax.shard_map(
        by_head if heads_fit else general_body,
        mesh=mesh,
        in_specs=(
            P("segment", "dev", None),
            P("segment", None),
            P("segment", None, "dev"),
            P("segment", None, "dev"),
            P("segment", None, "dev"),
            P("segment", None, "dev"),
            P("segment", "dev", None, None),
            P(),
            P("segment", "dev", None),
            P("segment", "dev"),
        ),
        out_specs=P("segment", "dev", None),
        check_vma=False,
    )
```

```python
import functools

import jax
import jax.numpy as jnp
from jax import lax
from jax.experimental import pallas as pl
from jax.experimental.pallas import tpu as pltpu
from jax.sharding import PartitionSpec as P

HEADS = 32
KV_HEADS = 4
HEAD_DIM = 128


far_below = -1e30
norm_eps = 1e-05


def passed_along(shard, axis, by):
    size = lax.axis_size(axis)
    return lax.ppermute(shard, axis, [(i, (i + by) % size) for i in range(size)])


def lookup_slots(block_ids, block_slot):
    table_width = block_slot.shape[0]
    matches = block_ids[..., None] == jnp.arange(table_width, dtype=jnp.int32)
    return jnp.sum(jnp.where(matches, block_slot, 0), axis=-1)


def block_stats(scores, valid):
    block_top = jnp.max(scores, axis=-1)
    weights = jnp.exp(scores - block_top[..., None])
    block_total = jnp.sum(weights, axis=-1)
    live_mask = valid[:, None, None, None]
    block_top = jnp.where(live_mask, block_top, far_below)
    block_total = jnp.where(live_mask, block_total, 0.0)
    return (block_top, block_total, weights.astype(jnp.bfloat16))


def self_stats(queries, key_rows, value_rows, score_scale):
    scores = (
        jnp.einsum("qhgd,khd->qhgk", queries, key_rows, preferred_element_type=jnp.float32)
        * score_scale
    )
    row_count = queries.shape[0]
    causal = (jnp.arange(row_count)[None, :] <= jnp.arange(row_count)[:, None])[:, None, None, :]
    own_top = jnp.max(jnp.where(causal, scores, far_below), axis=-1)
    weights = jnp.where(causal, jnp.exp(scores - own_top[..., None]), 0.0)
    own_total = jnp.sum(weights, axis=-1)
    own_acc = jnp.einsum(
        "qhgk,khd->qhgd",
        weights.astype(jnp.bfloat16),
        value_rows,
        preferred_element_type=jnp.float32,
    )
    return (own_top, own_total, own_acc)


def combine_terms(block_top, block_total, block_acc, own_top, own_total, own_acc):
    row_peak = jnp.maximum(own_top, jnp.max(block_top, axis=0))
    block_scale = jnp.exp(block_top - row_peak)
    own_scale = jnp.exp(own_top - row_peak)
    numerator = own_acc * own_scale[..., None] + jnp.sum(block_acc * block_scale[..., None], axis=0)
    denominator = own_total * own_scale + jnp.sum(block_total * block_scale, axis=0)
    return (numerator / denominator[..., None]).astype(jnp.bfloat16)


def general_body(hidden, gain, w_query, w_key, w_value, w_out, cache, block_slot, retrieved, counts):
    devices = lax.axis_size("dev")
    owner_index = lax.axis_index("dev")
    group_size = HEADS // KV_HEADS
    score_scale = HEAD_DIM ** (-0.5)
    pair_width = KV_HEADS * HEAD_DIM
    query_width = HEADS * HEAD_DIM
    state = hidden[0].astype(jnp.float32)
    inverse = lax.rsqrt(jnp.mean(state * state, axis=-1, keepdims=True) + norm_eps)
    normed = (state * inverse * gain[0]).astype(jnp.bfloat16)
    stacked = jnp.concatenate([w_query[0], w_key[0], w_value[0]], axis=1)
    query_cols = w_query.shape[2]
    key_cols = w_key.shape[2]
    projected = jnp.dot(
        lax.all_gather(normed, "dev", axis=0, tiled=True),
        stacked,
        preferred_element_type=jnp.float32,
    ).astype(jnp.bfloat16)
    query_part = projected[:, :query_cols]
    key_part = projected[:, query_cols : query_cols + key_cols]
    value_part = projected[:, query_cols + key_cols :]
    query_flat, key_flat, value_flat = (
        lax.all_to_all(query_part, "dev", split_axis=0, concat_axis=1, tiled=True),
        lax.all_to_all(key_part, "dev", split_axis=0, concat_axis=1, tiled=True),
        lax.all_to_all(value_part, "dev", split_axis=0, concat_axis=1, tiled=True),
    )
    question = query_flat.shape[0]
    queries = query_flat.reshape(question, KV_HEADS, group_size, HEAD_DIM)
    own_keys = key_flat.reshape(question, KV_HEADS, HEAD_DIM)
    own_values = value_flat.reshape(question, KV_HEADS, HEAD_DIM)
    all_ids, all_counts = (
        lax.all_gather(retrieved[0], "dev", axis=0, tiled=True),
        lax.all_gather(counts[0], "dev", axis=0, tiled=True),
    )
    table_rows = cache.shape[1]
    slot_ids = lookup_slots(all_ids, block_slot)
    listed = jnp.arange(all_ids.shape[1], dtype=jnp.int32)[None, :] < all_counts[:, None]
    mine = listed & (slot_ids // table_rows == owner_index)
    local_row = slot_ids % table_rows
    picked = jnp.sum(
        (
            mine[:, :, None] & (local_row[:, :, None] == jnp.arange(table_rows, dtype=jnp.int32))
        ).astype(jnp.bfloat16),
        axis=1,
    )
    selected = jnp.einsum(
        "rb,btc->rtc", picked, cache[0], preferred_element_type=jnp.float32
    ).astype(jnp.bfloat16)
    own_top, own_total, own_acc = self_stats(queries, own_keys, own_values, score_scale)
    my_slots = lookup_slots(retrieved[0][0], block_slot)
    my_listed = jnp.arange(retrieved.shape[2], dtype=jnp.int32) < counts[0][0]
    owner_ids = jnp.arange(devices, dtype=jnp.int32)
    holders = jnp.any(
        my_listed[None, :] & (my_slots[None, :] // table_rows == owner_ids[:, None]), axis=1
    )
    arrived = lax.all_to_all(selected, "dev", split_axis=0, concat_axis=0, tiled=True)
    arrived_keys = arrived[:, :, :pair_width].reshape(devices, -1, KV_HEADS, HEAD_DIM)
    arrived_values = arrived[:, :, pair_width:].reshape(devices, -1, KV_HEADS, HEAD_DIM)
    scores = (
        jnp.einsum("qhgd,tbhd->tqhgb", queries, arrived_keys, preferred_element_type=jnp.float32)
        * score_scale
    )
    block_top, block_total, weights = block_stats(scores, holders)
    block_acc = jnp.einsum(
        "tqhgb,tbhd->tqhgd", weights, arrived_values, preferred_element_type=jnp.float32
    )
    block_acc = jnp.where(holders[:, None, None, None, None], block_acc, 0.0)
    context = combine_terms(block_top, block_total, block_acc, own_top, own_total, own_acc).reshape(
        question, query_width
    )
    branch_cols = jnp.dot(
        lax.all_gather(context, "dev", axis=0, tiled=True),
        w_out[0],
        preferred_element_type=jnp.float32,
    )
    branch = lax.all_to_all(branch_cols, "dev", split_axis=0, concat_axis=1, tiled=True)
    updated = (state + branch).astype(jnp.bfloat16)
    return passed_along(updated[None], "segment", 1)


CORES = 2
TAIL = 16
VMEM = pl.BlockSpec(memory_space=pltpu.VMEM)
SMEM = pl.BlockSpec(memory_space=pltpu.SMEM)
ANYWHERE = pl.BlockSpec(memory_space=pl.ANY)
HBM = pl.BlockSpec(memory_space=pltpu.HBM)
MIB = 1 << 20


def to_pair(x, k):
    size = lax.axis_size("dev")
    return lax.ppermute(x, "dev", [(d, d ^ (CORES * k)) for d in range(size)])


def to_partner(x):
    return lax.ppermute(x, "dev", [(d, d ^ 1) for d in range(lax.axis_size("dev"))])


def from_all(x):
    arrived = [x] + [to_pair(x, k) for k in range(1, KV_HEADS)]
    return [p for a in arrived for p in (a, to_partner(a))]


def after(x, *others):
    return lax.optimization_barrier((x, *others))[0]


def in_vmem(x):
    return pltpu.with_memory_space_constraint(x, pltpu.VMEM)


def my_place():
    me = lax.axis_index("dev")
    return me, me // CORES, lax.rem(me, CORES)


def matmul(a, b, dims=((1,), (0,))):
    return lax.dot_general(a, b, (dims, ((), ())), preferred_element_type=jnp.float32)


def load_kernel(count, *refs):
    sources, targets, sems = refs[:count], refs[count : 2 * count], refs[2 * count]
    copies = []
    for i in range(count):
        parts = sems.shape[1]
        depth = targets[i].shape[0] // parts
        for j in range(parts):
            rows = pl.ds(j * depth, depth)
            source = sources[i].at[rows] if len(sources[i].shape) == 2 else sources[i].at[0, rows]
            copies.append(pltpu.make_async_copy(source, targets[i].at[rows], sems.at[i, j]))
    for copy in copies:
        copy.start()
    for copy in copies:
        copy.wait()


def load(*arrays):
    return pl.pallas_call(
        functools.partial(load_kernel, len(arrays)),
        out_shape=[pltpu.VMEM(a.shape[-2:], a.dtype) for a in arrays],
        in_specs=[HBM] * len(arrays),
        out_specs=[VMEM] * len(arrays),
        scratch_shapes=[pltpu.SemaphoreType.DMA((len(arrays), 4))],
        compiler_params=pltpu.CompilerParams(vmem_limit_bytes=2 * MIB),
        cost_estimate=pl.CostEstimate(flops=0, bytes_accessed=0, transcendentals=0),
        name="load",
    )(*[pltpu.with_memory_space_constraint(a, pltpu.HBM) for a in arrays])


def pack_kernel(counts, other_counts, table_in, retrieved_in, cache, other_in, *rest):
    outs, (whole, table, retrieved, other, sems, list_sems) = rest[:-6], rest[-6:]
    lists = [
        pltpu.make_async_copy(source, target, list_sems.at[i])
        for i, (source, target) in enumerate(
            ((table_in, table), (retrieved_in, retrieved), (other_in, other))
        )
    ]
    for copy in lists:
        copy.start()
    lines, tokens = whole.shape[0], whole.shape[1]
    width = whole.shape[2] // 2
    copies = [
        pltpu.make_async_copy(cache.at[0, line], whole.at[line], sems.at[line]) for line in range(lines)
    ]
    for copy in copies:
        copy.start()
    for copy in lists:
        copy.wait()
    listed = retrieved.shape[2]
    lane = lax.broadcasted_iota(jnp.int32, (TAIL // 2, HEAD_DIM), 1)
    notes = []
    for ids, count in ((retrieved, counts), (other, other_counts)):
        note = jnp.where(lane == listed, count[0, 0], 0)
        for k in range(listed):
            note = jnp.where(lane == k, table[ids[0, 0, k]], note)
        notes.append(note.astype(jnp.float32))
    note = jnp.concatenate(notes, axis=0).astype(jnp.bfloat16)
    for out in outs[:-1]:
        out[out.shape[0] - TAIL :, :] = note
    split = outs[-2].shape[0] - TAIL
    targets = [(0, outs[0]), (1, outs[1]), (3, outs[2]), (2, outs[3])]
    for line in range(lines):
        copies[line].wait()
        for k, whole_out in targets:
            head = lax.bitwise_xor(my_place()[1], k)
            for part in range(2):
                columns = pl.ds(pl.multiple_of(part * width + head * HEAD_DIM, HEAD_DIM), HEAD_DIM)
                at, out = (line * 2 + part) * tokens, whole_out
                if k == 2 and at >= split:
                    at, out = at - split, outs[-1]
                out[at : at + tokens, :] = whole[line, :, columns]


def pack(table, retrieved, counts, other_retrieved, other_counts, cache):
    rows, tokens = cache.shape[1], cache.shape[2]
    full = rows * 2 * tokens
    early = full // tokens * 5 // 8 * tokens
    return pl.pallas_call(
        pack_kernel,
        out_shape=[
            pltpu.VMEM((height, HEAD_DIM), cache.dtype)
            for height in [full + TAIL] * (KV_HEADS - 1) + [early + TAIL, full - early]
        ],
        in_specs=[SMEM] * 2 + [HBM] * 3 + [ANYWHERE],
        out_specs=[VMEM] * (KV_HEADS + 1),
        scratch_shapes=[
            pltpu.VMEM(cache.shape[1:], cache.dtype),
            pltpu.SMEM(table.shape, table.dtype),
            pltpu.SMEM(retrieved.shape, retrieved.dtype),
            pltpu.SMEM(retrieved.shape, retrieved.dtype),
            pltpu.SemaphoreType.DMA((rows,)),
            pltpu.SemaphoreType.DMA((3,)),
        ],
        compiler_params=pltpu.CompilerParams(vmem_limit_bytes=6 * MIB),
        cost_estimate=pl.CostEstimate(flops=0, bytes_accessed=0, transcendentals=0),
        name="pack",
    )(
        counts,
        other_counts,
        *[pltpu.with_memory_space_constraint(a, pltpu.HBM) for a in (table, retrieved, cache)],
        other_retrieved,
    )


def project_kernel(*refs):
    count = 2 * KV_HEADS
    parts, rest = refs[:count], refs[count:]
    gain, wk, wv, normed, kv_out, cols_out = rest
    _, pair, core = my_place()
    first = core == 0
    width = cols_out.shape[1]
    columns = pl.ds(pl.multiple_of((CORES * pair + core) * width, 128), width)
    for k in range(KV_HEADS):
        source = lax.bitwise_xor(pair, k)
        rows = pl.ds(pl.multiple_of(source * 16, 16), 16)

        def both(at):
            a, b = (parts[2 * k + p][:, at].astype(jnp.float32) for p in range(CORES))
            return jnp.concatenate([jnp.where(first, a, b), jnp.where(first, b, a)], axis=0)

        state = both(slice(None))
        inverse = lax.rsqrt(jnp.mean(state * state, axis=-1, keepdims=True) + norm_eps)
        normed[rows, :] = (state * inverse * gain[...]).astype(jnp.bfloat16)
        cols_out[rows, :] = both(columns).astype(cols_out.dtype)
    key = matmul(normed[...], wk[...], ((1,), (1,)))
    value = matmul(normed[...], wv[...], ((1,), (1,)))
    kv_out[...] = jnp.concatenate([key, value], axis=1).astype(kv_out.dtype)


def project(parts, gain, wk, wv):
    tokens = sum(p.shape[0] for p in parts)
    width = parts[0].shape[1]
    bf16 = jnp.bfloat16
    return pl.pallas_call(
        project_kernel,
        out_shape=[
            pltpu.VMEM((tokens, width), bf16),
            pltpu.VMEM((tokens, 2 * wk.shape[0]), bf16),
            pltpu.VMEM((tokens, width // len(parts)), bf16),
        ],
        in_specs=[VMEM] * (len(parts) + 3),
        out_specs=[VMEM] * 3,
        compiler_params=pltpu.CompilerParams(vmem_limit_bytes=12 * MIB),
        cost_estimate=pl.CostEstimate(
            flops=0, bytes_accessed=0, transcendentals=0
        ),
        name="project",
    )(*[in_vmem(p) for p in parts], gain, in_vmem(wk), in_vmem(wv))


def query_kernel(normed, wq, out):
    out[...] = matmul(normed[...], wq[...]).astype(out.dtype)


def query(normed, wq):
    return pl.pallas_call(
        query_kernel,
        out_shape=pltpu.VMEM((normed.shape[0], wq.shape[1]), jnp.bfloat16),
        in_specs=[VMEM] * 2,
        out_specs=VMEM,
        compiler_params=pltpu.CompilerParams(vmem_limit_bytes=12 * MIB),
        cost_estimate=pl.CostEstimate(
            flops=0, bytes_accessed=0, transcendentals=0
        ),
        name="query",
    )(in_vmem(normed), in_vmem(wq))


def attend_kernel(listed, requests, q_mine, q_other, kv_mine, kv_other, *refs):
    *held, late = refs[: KV_HEADS + 1]
    mine, give, scored, notes, meta, line_of, live_of, joined, note_sem, sems = refs[KV_HEADS + 1 :]
    early = held[2].shape[0] - TAIL
    copies = [
        pltpu.make_async_copy(held[2].at[pl.ds(0, early)], joined.at[pl.ds(0, early)], sems.at[0]),
        pltpu.make_async_copy(late, joined.at[pl.ds(early, late.shape[0])], sems.at[1]),
    ]
    for copy in copies:
        copy.start()
    tokens = q_mine.shape[0]
    question = tokens // requests
    heads = q_mine.shape[1] // HEAD_DIM
    group = heads * question
    block = scored.shape[3]
    end = held[0].shape[0] - TAIL
    rows = end // (2 * block)
    me, pair, core = my_place()
    tails = [h[h.shape[0] - TAIL :, :].astype(jnp.float32) for h in held]
    held[2] = joined
    notes[...] = jnp.concatenate(
        [tail[at : at + 1] for tail in tails for at in (0, TAIL // 2)], axis=0
    ).astype(jnp.int32)
    noted = pltpu.make_async_copy(notes, meta, note_sem)
    noted.start()
    scale = HEAD_DIM ** (-0.5)
    first = core == 0
    half = HEAD_DIM // 2
    a, b = kv_mine[...].astype(jnp.float32), kv_other[...].astype(jnp.float32)
    lo, hi = jnp.where(first, a, b), jnp.where(first, b, a)
    own_key = jnp.concatenate([lo[:, :half], hi[:, :half]], axis=1).astype(jnp.bfloat16)
    own_value = jnp.concatenate([lo[:, half:], hi[:, half:]], axis=1).astype(jnp.bfloat16)
    wide = [q_mine[...].astype(jnp.float32), q_other[...].astype(jnp.float32)]

    def rows_of(side, r):
        piece = wide[side][r * question : (r + 1) * question]
        return [piece[:, h * HEAD_DIM : (h + 1) * HEAD_DIM] for h in range(heads)]

    queries = [
        jnp.concatenate(rows_of(0, r) + rows_of(1, r), axis=0).astype(jnp.bfloat16)
        for r in range(requests)
    ]
    stacked = jnp.concatenate([query[:group] for query in queries], axis=0)
    scores = matmul(stacked, own_key, ((1,), (1,))) * scale
    row = lax.broadcasted_iota(jnp.int32, scores.shape, 0)
    column = lax.broadcasted_iota(jnp.int32, scores.shape, 1)
    seen = (row // group == column // question) & (column % question <= row % question)
    own_top = jnp.max(jnp.where(seen, scores, far_below), axis=-1, keepdims=True)
    weights = jnp.where(seen, jnp.exp(scores - own_top), 0.0)
    own_total = jnp.sum(weights, axis=-1, keepdims=True)
    own_acc = matmul(weights.astype(jnp.bfloat16), own_value)
    for i in range(requests * KV_HEADS):
        line_of[i] = 0
        live_of[i] = 0
    noted.wait()
    for r in range(requests):
        at = lax.bitwise_xor(me, r)
        live = meta[at, listed]
        for k in range(listed):
            slot = meta[at, k]
            owner = lax.div(slot, rows)
            away = lax.bitwise_xor(lax.div(owner, CORES), pair)
            i = jnp.where(lax.rem(owner, CORES) == core, r * KV_HEADS + away, requests * KV_HEADS)
            line_of[i] = lax.rem(slot, rows)
            live_of[i] = (k < live).astype(jnp.int32)
    for copy in copies:
        copy.wait()
    for r in range(requests):
        for j in range(KV_HEADS):
            at = pl.multiple_of(line_of[r * KV_HEADS + j] * 2 * block, block)
            scored[r, j] = matmul(queries[r], held[j][pl.ds(at, block), :], ((1,), (1,))) * scale
    scores = scored[...]
    tops = jnp.max(scores, axis=-1, keepdims=True)
    weights = jnp.exp(scores - tops)
    totals = jnp.sum(weights, axis=-1, keepdims=True)
    scored[...] = weights
    lane = lax.broadcasted_iota(jnp.int32, (group, HEAD_DIM), 1)
    for r in range(requests):
        span = slice(r * group, (r + 1) * group)
        accs, marks, lives = [], [], []
        for j in range(KV_HEADS):
            at = pl.multiple_of(line_of[r * KV_HEADS + j] * 2 * block + block, block)
            accs.append(matmul(scored[r, j].astype(jnp.bfloat16), held[j][pl.ds(at, block), :]))
            lives.append(live_of[r * KV_HEADS + j] > 0)
            marks.append(jnp.where(lives[j], tops[r, j], far_below))
        highest = functools.reduce(jnp.maximum, marks)
        for side, out in enumerate((mine, give)):
            part = slice(side * group, (side + 1) * group)
            peak = highest[part]
            if side == 0:
                peak = jnp.maximum(peak, own_top[span])
                factor = jnp.exp(own_top[span] - peak)
                numerator, denominator = own_acc[span] * factor, own_total[span] * factor
            else:
                numerator, denominator = jnp.zeros((group, HEAD_DIM), jnp.float32), jnp.zeros_like(peak)
            for j in range(KV_HEADS):
                factor = jnp.where(lives[j], jnp.exp(marks[j][part] - peak), 0.0)
                numerator = numerator + accs[j][part] * factor
                denominator = denominator + totals[r, j][part] * factor
            out[span, :] = numerator
            stats = slice(requests * group + r * group, requests * group + (r + 1) * group)
            out[stats, :] = jnp.where(lane == 0, peak, denominator)


def attend(q_mine, q_other, kv_mine, kv_other, held, requests, listed, block):
    rows = q_mine.size // HEAD_DIM
    shape = pltpu.VMEM((2 * rows, HEAD_DIM), jnp.float32)
    return pl.pallas_call(
        functools.partial(attend_kernel, listed, requests),
        out_shape=[shape] * 2,
        in_specs=[VMEM] * (4 + len(held)),
        out_specs=[VMEM] * 2,
        scratch_shapes=[
            pltpu.VMEM((requests, KV_HEADS, 2 * rows // requests, block), jnp.float32),
            pltpu.VMEM((requests, HEAD_DIM), jnp.int32),
            pltpu.SMEM((requests, HEAD_DIM), jnp.int32),
            pltpu.SMEM((requests * KV_HEADS + 1,), jnp.int32),
            pltpu.SMEM((requests * KV_HEADS + 1,), jnp.int32),
            pltpu.VMEM((held[0].shape[0] - TAIL, HEAD_DIM), jnp.bfloat16),
            pltpu.SemaphoreType.DMA,
            pltpu.SemaphoreType.DMA((2,)),
        ],
        compiler_params=pltpu.CompilerParams(vmem_limit_bytes=12 * MIB),
        cost_estimate=pl.CostEstimate(
            flops=1 << 28, bytes_accessed=2 * MIB, transcendentals=1 << 18
        ),
        name="attend",
    )(*[in_vmem(a) for a in (q_mine, q_other, kv_mine, kv_other, *held)])


def merge_kernel(requests, mine, got, out, placed):
    rows = mine.shape[0] // 2
    question = out.shape[0] // requests
    heads = out.shape[1] // HEAD_DIM
    (sum_a, stat_a), (sum_b, stat_b) = ((a[:rows, :], a[rows:, :]) for a in (mine, got))
    peak = jnp.maximum(stat_a[:, :1], stat_b[:, :1])
    factor_a, factor_b = jnp.exp(stat_a[:, :1] - peak), jnp.exp(stat_b[:, :1] - peak)
    total = stat_a[:, 1:2] * factor_a + stat_b[:, 1:2] * factor_b
    context = (sum_a * factor_a + sum_b * factor_b) / total
    for r in range(requests):
        for h in range(heads):
            at = (r * heads + h) * question
            placed[r * question : (r + 1) * question, h * HEAD_DIM : (h + 1) * HEAD_DIM] = context[
                at : at + question
            ]
    out[...] = placed[...].astype(out.dtype)


def merge(mine, got, requests, q):
    return pl.pallas_call(
        functools.partial(merge_kernel, requests),
        out_shape=pltpu.VMEM(q.shape, jnp.bfloat16),
        in_specs=[VMEM] * 2,
        out_specs=VMEM,
        scratch_shapes=[pltpu.VMEM(q.shape, jnp.float32)],
        compiler_params=pltpu.CompilerParams(vmem_limit_bytes=6 * MIB),
        name="merge",
    )(in_vmem(mine), in_vmem(got))


def partial_kernel(*refs):
    parts, (w_out, out) = refs[:-2], refs[-2:]
    me, _, _ = my_place()
    depth = parts[0].shape[1]
    total = None
    for i, part in enumerate(parts):
        source = lax.bitwise_xor(me, i)
        span = pl.ds(pl.multiple_of(source * depth, depth), depth)
        product = matmul(part[...], w_out[span, :])
        total = product if total is None else total + product
    out[...] = total


def partial_branch(parts, w_out):
    tokens, width = parts[0].shape[0], w_out.shape[1]
    return pl.pallas_call(
        partial_kernel,
        out_shape=pltpu.VMEM((tokens, width), jnp.float32),
        in_specs=[VMEM] * (len(parts) + 1),
        out_specs=VMEM,
        compiler_params=pltpu.CompilerParams(vmem_limit_bytes=12 * MIB),
        cost_estimate=pl.CostEstimate(
            flops=tokens * w_out.size, bytes_accessed=w_out.size, transcendentals=0
        ),
        name="partial",
    )(*[in_vmem(p) for p in parts], in_vmem(w_out))


def away(turn, core):
    return lax.bitwise_xor(3 * (1 - turn), core)


def finish_kernel(*refs):
    parts, (before, cols, w_out, *outs, placed) = refs[:-6], refs[-6:]
    me, pair, core = my_place()
    depth = parts[0].shape[1]
    total = before[...]
    for i, part in enumerate(parts):
        source = lax.bitwise_xor(me, 2 * KV_HEADS - len(parts) + i)
        span = pl.ds(pl.multiple_of(source * depth, depth), depth)
        total = total + matmul(part[...], w_out[span, :])
    placed[...] = cols[...].astype(jnp.float32) + total
    keep, give = outs
    rows = keep.shape[0] // 2
    for k in range(KV_HEADS):
        target = lax.bitwise_xor(pair, away(k % 2, lax.bitwise_xor(core, k // 2)))
        piece = placed[pl.ds(pl.multiple_of(target * rows, rows), rows), :]
        out = (keep, give)[k // 2]
        out[k % 2 * rows : (k % 2 + 1) * rows, :] = piece.astype(out.dtype)


def finish(parts, before, cols, w_out):
    tokens, width = cols.shape
    shape = pltpu.VMEM((tokens // 2, width), jnp.bfloat16)
    return pl.pallas_call(
        finish_kernel,
        out_shape=[shape] * 2,
        in_specs=[VMEM] * (len(parts) + 3),
        out_specs=[VMEM] * 2,
        scratch_shapes=[pltpu.VMEM((tokens, width), jnp.float32)],
        compiler_params=pltpu.CompilerParams(vmem_limit_bytes=12 * MIB),
        cost_estimate=pl.CostEstimate(
            flops=tokens * w_out.size, bytes_accessed=w_out.size, transcendentals=0
        ),
        name="finish",
    )(*[in_vmem(p) for p in parts], in_vmem(before), in_vmem(cols), in_vmem(w_out))


def join_kernel(keep, got, *outs):
    rows = keep.shape[0] // 2
    for k, out in enumerate(outs):
        out[0] = keep[k * rows : (k + 1) * rows, :]
        out[1] = got[k * rows : (k + 1) * rows, :]


def join(keep, got):
    rows, width = keep.shape
    return pl.pallas_call(
        join_kernel,
        out_shape=[pltpu.VMEM((CORES, rows // 2, width), keep.dtype)] * 2,
        in_specs=[VMEM] * 2,
        out_specs=[VMEM] * 2,
        compiler_params=pltpu.CompilerParams(vmem_limit_bytes=4 * MIB),
        name="join",
    )(in_vmem(keep), in_vmem(got))


def place_kernel(*refs):
    parts, out = refs[:-1], refs[-1]
    me, _, core = my_place()
    rows, width = out.shape[1], parts[0].shape[2]
    for i, part in enumerate(parts):
        taker = lax.bitwise_xor(core, i % 2)
        sender = lax.bitwise_xor(me - core + taker, CORES * away(i // 2, taker))
        for p in range(CORES):
            source = lax.bitwise_xor(sender, p)
            both = part[p].astype(jnp.float32)
            mine = jnp.where(core == 0, both[:rows], both[rows:])
            out[0, :, pl.ds(pl.multiple_of(source * width, width), width)] = mine.astype(out.dtype)


def place_columns(parts):
    cores, rows, width = parts[0].shape
    return pl.pallas_call(
        place_kernel,
        out_shape=jax.ShapeDtypeStruct((1, rows // CORES, width * cores * len(parts)), jnp.bfloat16),
        in_specs=[VMEM] * len(parts),
        out_specs=VMEM,
        compiler_params=pltpu.CompilerParams(vmem_limit_bytes=4 * MIB),
        name="place",
    )(*[in_vmem(part) for part in parts])


def by_head(hidden, gain, w_query, w_key, w_value, w_out, cache, block_slot, retrieved, counts):
    size, sections = lax.axis_size("dev"), lax.axis_size("segment")
    state = hidden[0]
    gathered = {2: to_pair(state, 2), 1: to_pair(state, 1)}
    packed = pack(block_slot, retrieved, counts, to_partner(retrieved), to_partner(counts), cache)
    weights = load(w_query, w_key[0].swapaxes(0, 1), w_value[0].swapaxes(0, 1))
    early = to_pair(packed[3], 2)
    gathered[2], packed = lax.optimization_barrier((gathered[2], packed))
    gathered[3] = to_pair(gathered[2], 1)
    late = to_pair(packed[4], 2)
    blocks = {3: to_pair(packed[2], 3)}
    near, gathered[1] = lax.optimization_barrier((packed[1], gathered[1]))
    blocks[1] = to_pair(near, 1)
    gathered[3], early, late = lax.optimization_barrier((gathered[3], early, late))
    mine, gathered, weights = lax.optimization_barrier((state, gathered, weights))
    wq, wk, wv = weights
    parts = [p for a in (mine, *(gathered[k] for k in (1, 2, 3))) for p in (a, to_partner(a))]
    normed, kv, cols = project(parts, gain, wk, wv)
    q = query(normed, wq)
    blocks, q = lax.optimization_barrier((blocks, q))
    held = [packed[0], blocks[1], early, blocks[3], late]
    mine, give = attend(
        q, to_partner(q), kv, to_partner(kv), held, size, retrieved.shape[2], cache.shape[2]
    )
    context = merge(mine, to_partner(give), size, q)
    contexts = {0: context, 2: to_pair(context, 2), 1: to_pair(context, 1)}
    contexts[3] = to_pair(contexts[2], 1)
    contexts = [p for k in range(KV_HEADS) for p in (contexts[k], to_partner(contexts[k]))]
    before = partial_branch(contexts[:4], w_out[0])
    keep, give = finish(contexts[4:], before, cols, w_out[0])
    final = []
    for k, piece in enumerate(join(keep, to_partner(give))):
        route = [
            (s * size + d, (s + 1) % sections * size + (d ^ (CORES * (3 * (1 - k) ^ d % CORES))))
            for s in range(sections)
            for d in range(size)
        ]
        piece = lax.ppermute(piece, ("segment", "dev"), route)
        final += [piece, to_partner(piece)]
    return place_columns(final)


def solution(mesh):
    heads_fit = mesh.shape["dev"] == CORES * KV_HEADS
    return jax.shard_map(
        by_head if heads_fit else general_body,
        mesh=mesh,
        in_specs=(
            P("segment", "dev", None),
            P("segment", None),
            P("segment", None, "dev"),
            P("segment", None, "dev"),
            P("segment", None, "dev"),
            P("segment", None, "dev"),
            P("segment", "dev", None, None),
            P(),
            P("segment", "dev", None),
            P("segment", "dev"),
        ),
        out_specs=P("segment", "dev", None),
        check_vma=False,
    )
```

```python
import functools

import jax
import jax.numpy as jnp
from jax import lax
from jax.experimental import pallas as pl
from jax.experimental.pallas import tpu as pltpu
from jax.sharding import PartitionSpec as P

HEADS = 32
KV_HEADS = 4
HEAD_DIM = 128


far_below = -1e30
norm_eps = 1e-05


def passed_along(shard, axis, by):
    size = lax.axis_size(axis)
    return lax.ppermute(shard, axis, [(i, (i + by) % size) for i in range(size)])


def lookup_slots(block_ids, block_slot):
    table_width = block_slot.shape[0]
    matches = block_ids[..., None] == jnp.arange(table_width, dtype=jnp.int32)
    return jnp.sum(jnp.where(matches, block_slot, 0), axis=-1)


def block_stats(scores, valid):
    block_top = jnp.max(scores, axis=-1)
    weights = jnp.exp(scores - block_top[..., None])
    block_total = jnp.sum(weights, axis=-1)
    live_mask = valid[:, None, None, None]
    block_top = jnp.where(live_mask, block_top, far_below)
    block_total = jnp.where(live_mask, block_total, 0.0)
    return (block_top, block_total, weights.astype(jnp.bfloat16))


def self_stats(queries, key_rows, value_rows, score_scale):
    scores = (
        jnp.einsum("qhgd,khd->qhgk", queries, key_rows, preferred_element_type=jnp.float32)
        * score_scale
    )
    row_count = queries.shape[0]
    causal = (jnp.arange(row_count)[None, :] <= jnp.arange(row_count)[:, None])[:, None, None, :]
    own_top = jnp.max(jnp.where(causal, scores, far_below), axis=-1)
    weights = jnp.where(causal, jnp.exp(scores - own_top[..., None]), 0.0)
    own_total = jnp.sum(weights, axis=-1)
    own_acc = jnp.einsum(
        "qhgk,khd->qhgd",
        weights.astype(jnp.bfloat16),
        value_rows,
        preferred_element_type=jnp.float32,
    )
    return (own_top, own_total, own_acc)


def combine_terms(block_top, block_total, block_acc, own_top, own_total, own_acc):
    row_peak = jnp.maximum(own_top, jnp.max(block_top, axis=0))
    block_scale = jnp.exp(block_top - row_peak)
    own_scale = jnp.exp(own_top - row_peak)
    numerator = own_acc * own_scale[..., None] + jnp.sum(block_acc * block_scale[..., None], axis=0)
    denominator = own_total * own_scale + jnp.sum(block_total * block_scale, axis=0)
    return (numerator / denominator[..., None]).astype(jnp.bfloat16)


def general_body(hidden, gain, w_query, w_key, w_value, w_out, cache, block_slot, retrieved, counts):
    devices = lax.axis_size("dev")
    owner_index = lax.axis_index("dev")
    group_size = HEADS // KV_HEADS
    score_scale = HEAD_DIM ** (-0.5)
    pair_width = KV_HEADS * HEAD_DIM
    query_width = HEADS * HEAD_DIM
    state = hidden[0].astype(jnp.float32)
    inverse = lax.rsqrt(jnp.mean(state * state, axis=-1, keepdims=True) + norm_eps)
    normed = (state * inverse * gain[0]).astype(jnp.bfloat16)
    stacked = jnp.concatenate([w_query[0], w_key[0], w_value[0]], axis=1)
    query_cols = w_query.shape[2]
    key_cols = w_key.shape[2]
    projected = jnp.dot(
        lax.all_gather(normed, "dev", axis=0, tiled=True),
        stacked,
        preferred_element_type=jnp.float32,
    ).astype(jnp.bfloat16)
    query_part = projected[:, :query_cols]
    key_part = projected[:, query_cols : query_cols + key_cols]
    value_part = projected[:, query_cols + key_cols :]
    query_flat, key_flat, value_flat = (
        lax.all_to_all(query_part, "dev", split_axis=0, concat_axis=1, tiled=True),
        lax.all_to_all(key_part, "dev", split_axis=0, concat_axis=1, tiled=True),
        lax.all_to_all(value_part, "dev", split_axis=0, concat_axis=1, tiled=True),
    )
    question = query_flat.shape[0]
    queries = query_flat.reshape(question, KV_HEADS, group_size, HEAD_DIM)
    own_keys = key_flat.reshape(question, KV_HEADS, HEAD_DIM)
    own_values = value_flat.reshape(question, KV_HEADS, HEAD_DIM)
    all_ids, all_counts = (
        lax.all_gather(retrieved[0], "dev", axis=0, tiled=True),
        lax.all_gather(counts[0], "dev", axis=0, tiled=True),
    )
    table_rows = cache.shape[1]
    slot_ids = lookup_slots(all_ids, block_slot)
    listed = jnp.arange(all_ids.shape[1], dtype=jnp.int32)[None, :] < all_counts[:, None]
    mine = listed & (slot_ids // table_rows == owner_index)
    local_row = slot_ids % table_rows
    picked = jnp.sum(
        (
            mine[:, :, None] & (local_row[:, :, None] == jnp.arange(table_rows, dtype=jnp.int32))
        ).astype(jnp.bfloat16),
        axis=1,
    )
    selected = jnp.einsum(
        "rb,btc->rtc", picked, cache[0], preferred_element_type=jnp.float32
    ).astype(jnp.bfloat16)
    own_top, own_total, own_acc = self_stats(queries, own_keys, own_values, score_scale)
    my_slots = lookup_slots(retrieved[0][0], block_slot)
    my_listed = jnp.arange(retrieved.shape[2], dtype=jnp.int32) < counts[0][0]
    owner_ids = jnp.arange(devices, dtype=jnp.int32)
    holders = jnp.any(
        my_listed[None, :] & (my_slots[None, :] // table_rows == owner_ids[:, None]), axis=1
    )
    arrived = lax.all_to_all(selected, "dev", split_axis=0, concat_axis=0, tiled=True)
    arrived_keys = arrived[:, :, :pair_width].reshape(devices, -1, KV_HEADS, HEAD_DIM)
    arrived_values = arrived[:, :, pair_width:].reshape(devices, -1, KV_HEADS, HEAD_DIM)
    scores = (
        jnp.einsum("qhgd,tbhd->tqhgb", queries, arrived_keys, preferred_element_type=jnp.float32)
        * score_scale
    )
    block_top, block_total, weights = block_stats(scores, holders)
    block_acc = jnp.einsum(
        "tqhgb,tbhd->tqhgd", weights, arrived_values, preferred_element_type=jnp.float32
    )
    block_acc = jnp.where(holders[:, None, None, None, None], block_acc, 0.0)
    context = combine_terms(block_top, block_total, block_acc, own_top, own_total, own_acc).reshape(
        question, query_width
    )
    branch_cols = jnp.dot(
        lax.all_gather(context, "dev", axis=0, tiled=True),
        w_out[0],
        preferred_element_type=jnp.float32,
    )
    branch = lax.all_to_all(branch_cols, "dev", split_axis=0, concat_axis=1, tiled=True)
    updated = (state + branch).astype(jnp.bfloat16)
    return passed_along(updated[None], "segment", 1)


CORES = 2
TAIL = 16
VMEM = pl.BlockSpec(memory_space=pltpu.VMEM)
SMEM = pl.BlockSpec(memory_space=pltpu.SMEM)
ANYWHERE = pl.BlockSpec(memory_space=pl.ANY)
HBM = pl.BlockSpec(memory_space=pltpu.HBM)
MIB = 1 << 20


def to_pair(x, k):
    size = lax.axis_size("dev")
    return lax.ppermute(x, "dev", [(d, d ^ (CORES * k)) for d in range(size)])


def to_partner(x):
    return lax.ppermute(x, "dev", [(d, d ^ 1) for d in range(lax.axis_size("dev"))])


def from_all(x):
    arrived = [x] + [to_pair(x, k) for k in range(1, KV_HEADS)]
    return [p for a in arrived for p in (a, to_partner(a))]


def after(x, *others):
    return lax.optimization_barrier((x, *others))[0]


def in_vmem(x):
    return pltpu.with_memory_space_constraint(x, pltpu.VMEM)


def my_place():
    me = lax.axis_index("dev")
    return me, me // CORES, lax.rem(me, CORES)


def matmul(a, b, dims=((1,), (0,))):
    return lax.dot_general(a, b, (dims, ((), ())), preferred_element_type=jnp.float32)


def load_kernel(count, *refs):
    sources, targets, sems = refs[:count], refs[count : 2 * count], refs[2 * count]
    copies = []
    for i in range(count):
        parts = sems.shape[1]
        depth = targets[i].shape[0] // parts
        for j in range(parts):
            rows = pl.ds(j * depth, depth)
            source = sources[i].at[rows] if len(sources[i].shape) == 2 else sources[i].at[0, rows]
            copies.append(pltpu.make_async_copy(source, targets[i].at[rows], sems.at[i, j]))
    for copy in copies:
        copy.start()
    for copy in copies:
        copy.wait()


def load(*arrays):
    return pl.pallas_call(
        functools.partial(load_kernel, len(arrays)),
        out_shape=[pltpu.VMEM(a.shape[-2:], a.dtype) for a in arrays],
        in_specs=[HBM] * len(arrays),
        out_specs=[VMEM] * len(arrays),
        scratch_shapes=[pltpu.SemaphoreType.DMA((len(arrays), 4))],
        compiler_params=pltpu.CompilerParams(vmem_limit_bytes=2 * MIB),
        cost_estimate=pl.CostEstimate(flops=0, bytes_accessed=0, transcendentals=0),
        name="load",
    )(*[pltpu.with_memory_space_constraint(a, pltpu.HBM) for a in arrays])


def pack_kernel(counts, other_counts, table_in, retrieved_in, cache, other_in, *rest):
    outs, (whole, table, retrieved, other, sems, list_sems) = rest[:-6], rest[-6:]
    lists = [
        pltpu.make_async_copy(source, target, list_sems.at[i])
        for i, (source, target) in enumerate(
            ((table_in, table), (retrieved_in, retrieved), (other_in, other))
        )
    ]
    for copy in lists:
        copy.start()
    lines, tokens = whole.shape[0], whole.shape[1]
    width = whole.shape[2] // 2
    copies = [
        pltpu.make_async_copy(cache.at[0, line], whole.at[line], sems.at[line]) for line in range(lines)
    ]
    for copy in copies:
        copy.start()
    for copy in lists:
        copy.wait()
    listed = retrieved.shape[2]
    lane = lax.broadcasted_iota(jnp.int32, (TAIL // 2, HEAD_DIM), 1)
    notes = []
    for ids, count in ((retrieved, counts), (other, other_counts)):
        note = jnp.where(lane == listed, count[0, 0], 0)
        for k in range(listed):
            note = jnp.where(lane == k, table[ids[0, 0, k]], note)
        notes.append(note.astype(jnp.float32))
    note = jnp.concatenate(notes, axis=0).astype(jnp.bfloat16)
    for out in outs[:-1]:
        out[out.shape[0] - TAIL :, :] = note
    split = outs[-2].shape[0] - TAIL
    targets = [(0, outs[0]), (1, outs[1]), (3, outs[2]), (2, outs[3])]
    for line in range(lines):
        copies[line].wait()
        for k, whole_out in targets:
            head = lax.bitwise_xor(my_place()[1], k)
            for part in range(2):
                columns = pl.ds(pl.multiple_of(part * width + head * HEAD_DIM, HEAD_DIM), HEAD_DIM)
                at, out = (line * 2 + part) * tokens, whole_out
                if k == 2 and at >= split:
                    at, out = at - split, outs[-1]
                out[at : at + tokens, :] = whole[line, :, columns]


def pack(table, retrieved, counts, other_retrieved, other_counts, cache):
    rows, tokens = cache.shape[1], cache.shape[2]
    full = rows * 2 * tokens
    early = full // tokens * 4 // 8 * tokens
    return pl.pallas_call(
        pack_kernel,
        out_shape=[
            pltpu.VMEM((height, HEAD_DIM), cache.dtype)
            for height in [full + TAIL] * (KV_HEADS - 1) + [early + TAIL, full - early]
        ],
        in_specs=[SMEM] * 2 + [HBM] * 3 + [ANYWHERE],
        out_specs=[VMEM] * (KV_HEADS + 1),
        scratch_shapes=[
            pltpu.VMEM(cache.shape[1:], cache.dtype),
            pltpu.SMEM(table.shape, table.dtype),
            pltpu.SMEM(retrieved.shape, retrieved.dtype),
            pltpu.SMEM(retrieved.shape, retrieved.dtype),
            pltpu.SemaphoreType.DMA((rows,)),
            pltpu.SemaphoreType.DMA((3,)),
        ],
        compiler_params=pltpu.CompilerParams(vmem_limit_bytes=6 * MIB),
        cost_estimate=pl.CostEstimate(flops=0, bytes_accessed=0, transcendentals=0),
        name="pack",
    )(
        counts,
        other_counts,
        *[pltpu.with_memory_space_constraint(a, pltpu.HBM) for a in (table, retrieved, cache)],
        other_retrieved,
    )


def project_kernel(*refs):
    count = 2 * KV_HEADS
    parts, rest = refs[:count], refs[count:]
    gain, wk, wv, normed, kv_out, cols_out = rest
    _, pair, core = my_place()
    first = core == 0
    width = cols_out.shape[1]
    columns = pl.ds(pl.multiple_of((CORES * pair + core) * width, 128), width)
    for k in range(KV_HEADS):
        source = lax.bitwise_xor(pair, k)
        rows = pl.ds(pl.multiple_of(source * 16, 16), 16)

        def both(at):
            a, b = (parts[2 * k + p][:, at].astype(jnp.float32) for p in range(CORES))
            return jnp.concatenate([jnp.where(first, a, b), jnp.where(first, b, a)], axis=0)

        state = both(slice(None))
        inverse = lax.rsqrt(jnp.mean(state * state, axis=-1, keepdims=True) + norm_eps)
        normed[rows, :] = (state * inverse * gain[...]).astype(jnp.bfloat16)
        cols_out[rows, :] = both(columns).astype(cols_out.dtype)
    key = matmul(normed[...], wk[...], ((1,), (1,)))
    value = matmul(normed[...], wv[...], ((1,), (1,)))
    kv_out[...] = jnp.concatenate([key, value], axis=1).astype(kv_out.dtype)


def project(parts, gain, wk, wv):
    tokens = sum(p.shape[0] for p in parts)
    width = parts[0].shape[1]
    bf16 = jnp.bfloat16
    return pl.pallas_call(
        project_kernel,
        out_shape=[
            pltpu.VMEM((tokens, width), bf16),
            pltpu.VMEM((tokens, 2 * wk.shape[0]), bf16),
            pltpu.VMEM((tokens, width // len(parts)), bf16),
        ],
        in_specs=[VMEM] * (len(parts) + 3),
        out_specs=[VMEM] * 3,
        compiler_params=pltpu.CompilerParams(vmem_limit_bytes=12 * MIB),
        cost_estimate=pl.CostEstimate(
            flops=0, bytes_accessed=0, transcendentals=0
        ),
        name="project",
    )(*[in_vmem(p) for p in parts], gain, in_vmem(wk), in_vmem(wv))


def query_kernel(normed, wq, out):
    out[...] = matmul(normed[...], wq[...]).astype(out.dtype)


def query(normed, wq):
    return pl.pallas_call(
        query_kernel,
        out_shape=pltpu.VMEM((normed.shape[0], wq.shape[1]), jnp.bfloat16),
        in_specs=[VMEM] * 2,
        out_specs=VMEM,
        compiler_params=pltpu.CompilerParams(vmem_limit_bytes=12 * MIB),
        cost_estimate=pl.CostEstimate(
            flops=0, bytes_accessed=0, transcendentals=0
        ),
        name="query",
    )(in_vmem(normed), in_vmem(wq))


def attend_kernel(listed, requests, q_mine, q_other, kv_mine, kv_other, *refs):
    *held, late = refs[: KV_HEADS + 1]
    mine, give, scored, notes, meta, line_of, live_of, joined, note_sem, sems = refs[KV_HEADS + 1 :]
    early = held[2].shape[0] - TAIL
    copies = [
        pltpu.make_async_copy(held[2].at[pl.ds(0, early)], joined.at[pl.ds(0, early)], sems.at[0]),
        pltpu.make_async_copy(late, joined.at[pl.ds(early, late.shape[0])], sems.at[1]),
    ]
    for copy in copies:
        copy.start()
    tokens = q_mine.shape[0]
    question = tokens // requests
    heads = q_mine.shape[1] // HEAD_DIM
    group = heads * question
    block = scored.shape[3]
    end = held[0].shape[0] - TAIL
    rows = end // (2 * block)
    me, pair, core = my_place()
    tails = [h[h.shape[0] - TAIL :, :].astype(jnp.float32) for h in held]
    held[2] = joined
    notes[...] = jnp.concatenate(
        [tail[at : at + 1] for tail in tails for at in (0, TAIL // 2)], axis=0
    ).astype(jnp.int32)
    noted = pltpu.make_async_copy(notes, meta, note_sem)
    noted.start()
    scale = HEAD_DIM ** (-0.5)
    first = core == 0
    half = HEAD_DIM // 2
    a, b = kv_mine[...].astype(jnp.float32), kv_other[...].astype(jnp.float32)
    lo, hi = jnp.where(first, a, b), jnp.where(first, b, a)
    own_key = jnp.concatenate([lo[:, :half], hi[:, :half]], axis=1).astype(jnp.bfloat16)
    own_value = jnp.concatenate([lo[:, half:], hi[:, half:]], axis=1).astype(jnp.bfloat16)
    wide = [q_mine[...].astype(jnp.float32), q_other[...].astype(jnp.float32)]

    def rows_of(side, r):
        piece = wide[side][r * question : (r + 1) * question]
        return [piece[:, h * HEAD_DIM : (h + 1) * HEAD_DIM] for h in range(heads)]

    queries = [
        jnp.concatenate(rows_of(0, r) + rows_of(1, r), axis=0).astype(jnp.bfloat16)
        for r in range(requests)
    ]
    stacked = jnp.concatenate([query[:group] for query in queries], axis=0)
    scores = matmul(stacked, own_key, ((1,), (1,))) * scale
    row = lax.broadcasted_iota(jnp.int32, scores.shape, 0)
    column = lax.broadcasted_iota(jnp.int32, scores.shape, 1)
    seen = (row // group == column // question) & (column % question <= row % question)
    own_top = jnp.max(jnp.where(seen, scores, far_below), axis=-1, keepdims=True)
    weights = jnp.where(seen, jnp.exp(scores - own_top), 0.0)
    own_total = jnp.sum(weights, axis=-1, keepdims=True)
    own_acc = matmul(weights.astype(jnp.bfloat16), own_value)
    for i in range(requests * KV_HEADS):
        line_of[i] = 0
        live_of[i] = 0
    noted.wait()
    for r in range(requests):
        at = lax.bitwise_xor(me, r)
        live = meta[at, listed]
        for k in range(listed):
            slot = meta[at, k]
            owner = lax.div(slot, rows)
            away = lax.bitwise_xor(lax.div(owner, CORES), pair)
            i = jnp.where(lax.rem(owner, CORES) == core, r * KV_HEADS + away, requests * KV_HEADS)
            line_of[i] = lax.rem(slot, rows)
            live_of[i] = (k < live).astype(jnp.int32)
    for copy in copies:
        copy.wait()
    for r in range(requests):
        for j in range(KV_HEADS):
            at = pl.multiple_of(line_of[r * KV_HEADS + j] * 2 * block, block)
            scored[r, j] = matmul(queries[r], held[j][pl.ds(at, block), :], ((1,), (1,))) * scale
    scores = scored[...]
    tops = jnp.max(scores, axis=-1, keepdims=True)
    weights = jnp.exp(scores - tops)
    totals = jnp.sum(weights, axis=-1, keepdims=True)
    scored[...] = weights
    lane = lax.broadcasted_iota(jnp.int32, (group, HEAD_DIM), 1)
    for r in range(requests):
        span = slice(r * group, (r + 1) * group)
        accs, marks, lives = [], [], []
        for j in range(KV_HEADS):
            at = pl.multiple_of(line_of[r * KV_HEADS + j] * 2 * block + block, block)
            accs.append(matmul(scored[r, j].astype(jnp.bfloat16), held[j][pl.ds(at, block), :]))
            lives.append(live_of[r * KV_HEADS + j] > 0)
            marks.append(jnp.where(lives[j], tops[r, j], far_below))
        highest = functools.reduce(jnp.maximum, marks)
        for side, out in enumerate((mine, give)):
            part = slice(side * group, (side + 1) * group)
            peak = highest[part]
            if side == 0:
                peak = jnp.maximum(peak, own_top[span])
                factor = jnp.exp(own_top[span] - peak)
                numerator, denominator = own_acc[span] * factor, own_total[span] * factor
            else:
                numerator, denominator = jnp.zeros((group, HEAD_DIM), jnp.float32), jnp.zeros_like(peak)
            for j in range(KV_HEADS):
                factor = jnp.where(lives[j], jnp.exp(marks[j][part] - peak), 0.0)
                numerator = numerator + accs[j][part] * factor
                denominator = denominator + totals[r, j][part] * factor
            out[span, :] = numerator
            stats = slice(requests * group + r * group, requests * group + (r + 1) * group)
            out[stats, :] = jnp.where(lane == 0, peak, denominator)


def attend(q_mine, q_other, kv_mine, kv_other, held, requests, listed, block):
    rows = q_mine.size // HEAD_DIM
    shape = pltpu.VMEM((2 * rows, HEAD_DIM), jnp.float32)
    return pl.pallas_call(
        functools.partial(attend_kernel, listed, requests),
        out_shape=[shape] * 2,
        in_specs=[VMEM] * (4 + len(held)),
        out_specs=[VMEM] * 2,
        scratch_shapes=[
            pltpu.VMEM((requests, KV_HEADS, 2 * rows // requests, block), jnp.float32),
            pltpu.VMEM((requests, HEAD_DIM), jnp.int32),
            pltpu.SMEM((requests, HEAD_DIM), jnp.int32),
            pltpu.SMEM((requests * KV_HEADS + 1,), jnp.int32),
            pltpu.SMEM((requests * KV_HEADS + 1,), jnp.int32),
            pltpu.VMEM((held[0].shape[0] - TAIL, HEAD_DIM), jnp.bfloat16),
            pltpu.SemaphoreType.DMA,
            pltpu.SemaphoreType.DMA((2,)),
        ],
        compiler_params=pltpu.CompilerParams(vmem_limit_bytes=12 * MIB),
        cost_estimate=pl.CostEstimate(
            flops=1 << 28, bytes_accessed=2 * MIB, transcendentals=1 << 18
        ),
        name="attend",
    )(*[in_vmem(a) for a in (q_mine, q_other, kv_mine, kv_other, *held)])


def merge_kernel(requests, mine, got, out, placed):
    rows = mine.shape[0] // 2
    question = out.shape[0] // requests
    heads = out.shape[1] // HEAD_DIM
    (sum_a, stat_a), (sum_b, stat_b) = ((a[:rows, :], a[rows:, :]) for a in (mine, got))
    peak = jnp.maximum(stat_a[:, :1], stat_b[:, :1])
    factor_a, factor_b = jnp.exp(stat_a[:, :1] - peak), jnp.exp(stat_b[:, :1] - peak)
    total = stat_a[:, 1:2] * factor_a + stat_b[:, 1:2] * factor_b
    context = (sum_a * factor_a + sum_b * factor_b) / total
    for r in range(requests):
        for h in range(heads):
            at = (r * heads + h) * question
            placed[r * question : (r + 1) * question, h * HEAD_DIM : (h + 1) * HEAD_DIM] = context[
                at : at + question
            ]
    out[...] = placed[...].astype(out.dtype)


def merge(mine, got, requests, q):
    return pl.pallas_call(
        functools.partial(merge_kernel, requests),
        out_shape=pltpu.VMEM(q.shape, jnp.bfloat16),
        in_specs=[VMEM] * 2,
        out_specs=VMEM,
        scratch_shapes=[pltpu.VMEM(q.shape, jnp.float32)],
        compiler_params=pltpu.CompilerParams(vmem_limit_bytes=6 * MIB),
        name="merge",
    )(in_vmem(mine), in_vmem(got))


def partial_kernel(*refs):
    parts, (w_out, out) = refs[:-2], refs[-2:]
    me, _, _ = my_place()
    depth = parts[0].shape[1]
    total = None
    for i, part in enumerate(parts):
        source = lax.bitwise_xor(me, i)
        span = pl.ds(pl.multiple_of(source * depth, depth), depth)
        product = matmul(part[...], w_out[span, :])
        total = product if total is None else total + product
    out[...] = total


def partial_branch(parts, w_out):
    tokens, width = parts[0].shape[0], w_out.shape[1]
    return pl.pallas_call(
        partial_kernel,
        out_shape=pltpu.VMEM((tokens, width), jnp.float32),
        in_specs=[VMEM] * (len(parts) + 1),
        out_specs=VMEM,
        compiler_params=pltpu.CompilerParams(vmem_limit_bytes=12 * MIB),
        cost_estimate=pl.CostEstimate(
            flops=tokens * w_out.size, bytes_accessed=w_out.size, transcendentals=0
        ),
        name="partial",
    )(*[in_vmem(p) for p in parts], in_vmem(w_out))


def away(turn, core):
    return lax.bitwise_xor(3 * (1 - turn), core)


def finish_kernel(*refs):
    parts, (before, cols, w_out, *outs, placed) = refs[:-6], refs[-6:]
    me, pair, core = my_place()
    depth = parts[0].shape[1]
    total = before[...]
    for i, part in enumerate(parts):
        source = lax.bitwise_xor(me, 2 * KV_HEADS - len(parts) + i)
        span = pl.ds(pl.multiple_of(source * depth, depth), depth)
        total = total + matmul(part[...], w_out[span, :])
    placed[...] = cols[...].astype(jnp.float32) + total
    keep, give = outs
    rows = keep.shape[0] // 2
    for k in range(KV_HEADS):
        target = lax.bitwise_xor(pair, away(k % 2, lax.bitwise_xor(core, k // 2)))
        piece = placed[pl.ds(pl.multiple_of(target * rows, rows), rows), :]
        out = (keep, give)[k // 2]
        out[k % 2 * rows : (k % 2 + 1) * rows, :] = piece.astype(out.dtype)


def finish(parts, before, cols, w_out):
    tokens, width = cols.shape
    shape = pltpu.VMEM((tokens // 2, width), jnp.bfloat16)
    return pl.pallas_call(
        finish_kernel,
        out_shape=[shape] * 2,
        in_specs=[VMEM] * (len(parts) + 3),
        out_specs=[VMEM] * 2,
        scratch_shapes=[pltpu.VMEM((tokens, width), jnp.float32)],
        compiler_params=pltpu.CompilerParams(vmem_limit_bytes=12 * MIB),
        cost_estimate=pl.CostEstimate(
            flops=tokens * w_out.size, bytes_accessed=w_out.size, transcendentals=0
        ),
        name="finish",
    )(*[in_vmem(p) for p in parts], in_vmem(before), in_vmem(cols), in_vmem(w_out))


def join_kernel(keep, got, *outs):
    rows = keep.shape[0] // 2
    for k, out in enumerate(outs):
        out[0] = keep[k * rows : (k + 1) * rows, :]
        out[1] = got[k * rows : (k + 1) * rows, :]


def join(keep, got):
    rows, width = keep.shape
    return pl.pallas_call(
        join_kernel,
        out_shape=[pltpu.VMEM((CORES, rows // 2, width), keep.dtype)] * 2,
        in_specs=[VMEM] * 2,
        out_specs=[VMEM] * 2,
        compiler_params=pltpu.CompilerParams(vmem_limit_bytes=4 * MIB),
        name="join",
    )(in_vmem(keep), in_vmem(got))


def place_kernel(*refs):
    parts, out = refs[:-1], refs[-1]
    me, _, core = my_place()
    rows, width = out.shape[1], parts[0].shape[2]
    for i, part in enumerate(parts):
        taker = lax.bitwise_xor(core, i % 2)
        sender = lax.bitwise_xor(me - core + taker, CORES * away(i // 2, taker))
        for p in range(CORES):
            source = lax.bitwise_xor(sender, p)
            both = part[p].astype(jnp.float32)
            mine = jnp.where(core == 0, both[:rows], both[rows:])
            out[0, :, pl.ds(pl.multiple_of(source * width, width), width)] = mine.astype(out.dtype)


def place_columns(parts):
    cores, rows, width = parts[0].shape
    return pl.pallas_call(
        place_kernel,
        out_shape=jax.ShapeDtypeStruct((1, rows // CORES, width * cores * len(parts)), jnp.bfloat16),
        in_specs=[VMEM] * len(parts),
        out_specs=VMEM,
        compiler_params=pltpu.CompilerParams(vmem_limit_bytes=4 * MIB),
        name="place",
    )(*[in_vmem(part) for part in parts])


def by_head(hidden, gain, w_query, w_key, w_value, w_out, cache, block_slot, retrieved, counts):
    size, sections = lax.axis_size("dev"), lax.axis_size("segment")
    state = hidden[0]
    gathered = {2: to_pair(state, 2), 1: to_pair(state, 1)}
    packed = pack(block_slot, retrieved, counts, to_partner(retrieved), to_partner(counts), cache)
    weights = load(w_query, w_key[0].swapaxes(0, 1), w_value[0].swapaxes(0, 1))
    early = to_pair(packed[3], 2)
    gathered[2], packed = lax.optimization_barrier((gathered[2], packed))
    gathered[3] = to_pair(gathered[2], 1)
    late = to_pair(packed[4], 2)
    blocks = {3: to_pair(packed[2], 3)}
    near, gathered[1] = lax.optimization_barrier((packed[1], gathered[1]))
    blocks[1] = to_pair(near, 1)
    gathered[3], early, late = lax.optimization_barrier((gathered[3], early, late))
    mine, gathered, weights = lax.optimization_barrier((state, gathered, weights))
    wq, wk, wv = weights
    parts = [p for a in (mine, *(gathered[k] for k in (1, 2, 3))) for p in (a, to_partner(a))]
    normed, kv, cols = project(parts, gain, wk, wv)
    q = query(normed, wq)
    blocks, q = lax.optimization_barrier((blocks, q))
    held = [packed[0], blocks[1], early, blocks[3], late]
    mine, give = attend(
        q, to_partner(q), kv, to_partner(kv), held, size, retrieved.shape[2], cache.shape[2]
    )
    context = merge(mine, to_partner(give), size, q)
    contexts = {0: context, 2: to_pair(context, 2), 1: to_pair(context, 1)}
    contexts[3] = to_pair(context, 3)
    contexts = [p for k in range(KV_HEADS) for p in (contexts[k], to_partner(contexts[k]))]
    before = partial_branch(contexts[:4], w_out[0])
    keep, give = finish(contexts[4:], before, cols, w_out[0])
    final = []
    for k, piece in enumerate(join(keep, to_partner(give))):
        route = [
            (s * size + d, (s + 1) % sections * size + (d ^ (CORES * (3 * (1 - k) ^ d % CORES))))
            for s in range(sections)
            for d in range(size)
        ]
        piece = lax.ppermute(piece, ("segment", "dev"), route)
        final += [piece, to_partner(piece)]
    return place_columns(final)


def solution(mesh):
    heads_fit = mesh.shape["dev"] == CORES * KV_HEADS
    return jax.shard_map(
        by_head if heads_fit else general_body,
        mesh=mesh,
        in_specs=(
            P("segment", "dev", None),
            P("segment", None),
            P("segment", None, "dev"),
            P("segment", None, "dev"),
            P("segment", None, "dev"),
            P("segment", None, "dev"),
            P("segment", "dev", None, None),
            P(),
            P("segment", "dev", None),
            P("segment", "dev"),
        ),
        out_specs=P("segment", "dev", None),
        check_vma=False,
    )
```
